128 devices in a mesh: dp: 2 (over z_lo), row: 8 (over x, z_hi), col: 8 (over y, core).
Axes of the slice: x: 4, y: 4, z: 4 (z_hi: 2, z_lo: 2; z = z_hi * 2 + z_lo), core: 2. Of those that a mesh axis runs over, the one named last changes fastest.
Arguments:
- tokens: bfloat16 [384, 8192], P('dp', 'row'), may hold values from -6 to 6
- token_tangent: bfloat16 [384, 8192], P('dp', 'row'), may hold values from -6 to 6
- gate_weight: bfloat16 [8192, 14336], P('row', ('dp', 'col')), may hold values from -0.0625 to 0.0625
- up_weight: bfloat16 [8192, 14336], P('row', ('dp', 'col')), may hold values from -0.0625 to 0.0625
- gate_delta: bfloat16 [8192, 14336], P('row', ('dp', 'col')), may hold values from -0.0625 to 0.0625
- up_delta: bfloat16 [8192, 14336], P('row', ('dp', 'col')), may hold values from -0.0625 to 0.0625
- down_weight: bfloat16 [14336, 8192], P(('dp', 'col'), 'row'), may hold values from -0.046875 to 0.046875
- down_delta: bfloat16 [14336, 8192], P(('dp', 'col'), 'row'), may hold values from -0.046875 to 0.046875
- cotangent: bfloat16 [384, 8192], P(('dp', 'col'), 'row'), may hold values from -6 to 6
Outputs:
- output_primal: bfloat16 [384, 8192], P(('dp', 'col'), 'row')
- output_tangent: bfloat16 [384, 8192], P(('dp', 'col'), 'row')
- input_cotangent: bfloat16 [384, 8192], P(('dp', 'col'), 'row')
- gate_gradient: bfloat16 [8192, 14336], P('row', ('dp', 'col'))
- up_gradient: bfloat16 [8192, 14336], P('row', ('dp', 'col'))
- down_gradient: bfloat16 [14336, 8192], P(('dp', 'col'), 'row')
The draws below stay inside these ranges and needn't reach their ends.
All inputs are finite; a program needn't handle non-finite values.
Results may differ from the reference program's by a relative error of at most 0.005.
Values may be sent and summed in bfloat16 or wider, within the bound.
A program may use at most 128 MiB of HBM per device.

```python
import math
import jax
import jax.numpy as jnp

D = 8192
FF = 14336
TOKENS = 384


def block_levels(key, dims, pieces, low, high):
    loudness, own = 1.0, jax.random.fold_in(key, 6)
    for position, parts in pieces:
        draws = jnp.exp(jax.random.uniform(jax.random.fold_in(own, position), (parts,), jnp.float32, low / len(pieces), high / len(pieces)))
        loudness = loudness * jnp.repeat(draws, dims[position] // parts).reshape([-1 if axis == position else 1 for axis in range(len(dims))])
    return loudness


def scatter_about(key, extent, scale, limit, shards=(), kind=jnp.bfloat16):
    loudness = block_levels(key, extent, shards, -0.22, 0.18) if shards else 1.0
    entries = jax.random.normal(key, extent, jnp.float32) * scale * loudness
    return jnp.minimum(jnp.maximum(entries, -limit), limit).astype(kind)


def setup_inputs(seed: int = 0) -> dict:
    splits = jax.random.split(jax.random.key(seed), 10)
    tokens = scatter_about(splits[0], (TOKENS, D), 1.0, 6.0, ((0, 2), (1, 8)))
    token_tangent = scatter_about(splits[1], (TOKENS, D), 1.0, 6.0, ((0, 2), (1, 8)))
    gate_weight = scatter_about(splits[2], (D, FF), D ** -0.5, 0.0625, ((0, 8), (1, 16)))
    up_weight = scatter_about(splits[3], (D, FF), D ** -0.5, 0.0625, ((0, 8), (1, 16)))
    gate_delta = scatter_about(splits[4], (D, FF), D ** -0.5, 0.0625, ((0, 8), (1, 16)))
    up_delta = scatter_about(splits[5], (D, FF), D ** -0.5, 0.0625, ((0, 8), (1, 16)))
    down_weight = scatter_about(splits[6], (FF, D), FF ** -0.5, 0.046875, ((0, 16), (1, 8)))
    down_delta = scatter_about(splits[7], (FF, D), FF ** -0.5, 0.046875, ((0, 16), (1, 8)))
    cotangent = scatter_about(splits[8], (TOKENS, D), 1.0, 6.0, ((0, 16), (1, 8)))
    return dict(tokens=tokens, token_tangent=token_tangent, gate_weight=gate_weight, up_weight=up_weight, gate_delta=gate_delta, up_delta=up_delta, down_weight=down_weight, down_delta=down_delta, cotangent=cotangent)


def silu_pair(gate_sum):
    logistic = jax.nn.sigmoid(gate_sum)
    return (gate_sum * logistic, logistic * (1.0 + gate_sum * (1.0 - logistic)))

def matmul(left_side, right_side):
    return jnp.dot(left_side, right_side, preferred_element_type=jnp.float32)

def reference(tokens, token_tangent, gate_weight, up_weight, gate_delta, up_delta, down_weight, down_delta, cotangent):
    gate_sum = matmul(tokens, gate_weight)
    up_sum = matmul(tokens, up_weight)
    gate_tangent = matmul(tokens, gate_delta) + matmul(token_tangent, gate_weight)
    up_tangent = matmul(tokens, up_delta) + matmul(token_tangent, up_weight)
    activation, derivative = silu_pair(gate_sum)
    hidden = (activation * up_sum).astype(jnp.bfloat16)
    hidden_tangent = (derivative * gate_tangent * up_sum + activation * up_tangent).astype(jnp.bfloat16)
    output_primal = matmul(hidden, down_weight).astype(jnp.bfloat16)
    output_tangent = (matmul(hidden_tangent, down_weight) + matmul(hidden, down_delta)).astype(jnp.bfloat16)
    back_sum = matmul(cotangent, down_weight.T)
    grad_gate = (back_sum * (up_sum * derivative)).astype(jnp.bfloat16)
    grad_up = (back_sum * activation).astype(jnp.bfloat16)
    input_cotangent = (matmul(grad_gate, gate_weight.T) + matmul(grad_up, up_weight.T)).astype(jnp.bfloat16)
    normalizer = 1.0 / math.sqrt(TOKENS)
    gate_gradient = (matmul(tokens.T, grad_gate) * normalizer).astype(jnp.bfloat16)
    up_gradient = (matmul(tokens.T, grad_up) * normalizer).astype(jnp.bfloat16)
    down_gradient = (matmul(hidden.T, cotangent) * normalizer).astype(jnp.bfloat16)
    return (output_primal, output_tangent, input_cotangent, gate_gradient, up_gradient, down_gradient)
```

```python
import functools
import math

import jax
import jax.numpy as jnp
from jax import lax
from jax.experimental import pallas as pl
from jax.experimental.pallas import tpu as pltpu
from jax.sharding import PartitionSpec as P

BF16 = jnp.bfloat16
F32 = jnp.float32
MESH = pl.DeviceIdType.MESH
TRANS_RIGHT = (((1,), (1,)), ((), ()))
TRANS_LEFT = (((0,), (0,)), ((), ()))


def dot(left_side, right_side):
    return jnp.dot(left_side, right_side, preferred_element_type=F32)


def dot_trans(left_side, right_side):
    return lax.dot_general(left_side, right_side, TRANS_RIGHT, preferred_element_type=F32)


class Copies:
    def __init__(self, send_sems, recv_sems, local_sems):
        self.send_sems, self.recv_sems, self.local_sems = send_sems, recv_sems, local_sems
        self.remote_count = 0
        self.local_count = 0
        self.sent = []

    def start(self, src, dst, device):
        k = self.remote_count
        self.remote_count += 1
        copy = pltpu.make_async_remote_copy(
            src_ref=src,
            dst_ref=dst,
            send_sem=self.send_sems.at[k],
            recv_sem=self.recv_sems.at[k],
            device_id=device,
            device_id_type=MESH,
        )
        copy.start()
        self.sent.append(copy)
        return copy

    def local(self, src, dst):
        k = self.local_count
        self.local_count += 1
        copy = pltpu.make_async_copy(src, dst, self.local_sems.at[k])
        copy.start()
        return copy


class RingSum:
    def __init__(self, copies, me, left, right, block, exact, sent, first, merged, from_left, from_right):
        self.copies, self.left, self.right = copies, left, right
        self.rows = lambda shift: pl.ds(pl.multiple_of(lax.rem(me + shift, 4) * block, 16), block)
        self.exact, self.packed, self.first, self.merged = exact, sent, first, merged
        self.from_left, self.from_right = from_left, from_right

    def start(self):
        far, after, before = self.rows(2), self.rows(1), self.rows(3)
        send = self.copies.start
        self.a0 = send(self.packed.at[0, far], self.first.at[0], self.right)
        self.a1 = send(self.packed.at[1, far], self.first.at[1], self.left)
        self.b1 = send(self.packed.at[1, after], self.from_left.at[1], self.right)
        self.b0 = send(self.packed.at[0, before], self.from_right.at[0], self.left)

    def merge(self):
        send = self.copies.start
        self.a0.wait_recv()
        self.merged[0] = (self.exact[0, self.rows(1)] + self.first[0].astype(F32)).astype(BF16)
        self.c0 = send(self.merged.at[0], self.from_left.at[0], self.right)
        self.a1.wait_recv()
        self.merged[1] = (self.exact[1, self.rows(3)] + self.first[1].astype(F32)).astype(BF16)
        self.c1 = send(self.merged.at[1], self.from_right.at[1], self.left)

    def wait(self):
        for copy in (self.b0, self.b1, self.c0, self.c1):
            copy.wait_recv()

    def total(self, plane):
        return (
            self.exact[plane, self.rows(0)]
            + self.from_left[plane].astype(F32)
            + self.from_right[plane].astype(F32)
        )


class RingGather:
    def __init__(self, copies, me, left, right, block, whole):
        self.copies, self.left, self.right, self.whole = copies, left, right, whole
        self.rows = lambda shift: pl.ds(pl.multiple_of(lax.rem(me + shift, 4) * block, 16), block)

    def send(self, plane, shift, device):
        part = self.whole.at[plane, self.rows(shift)]
        return self.copies.start(part, part, device)

    def start(self):
        self.a0 = self.send(0, 0, self.right)
        self.a1 = self.send(1, 0, self.left)
        self.b1 = self.send(1, 0, self.right)
        self.b0 = self.send(0, 0, self.left)

    def forward(self):
        self.a0.wait_recv()
        self.c0 = self.send(0, 3, self.right)
        self.a1.wait_recv()
        self.c1 = self.send(1, 1, self.left)

    def wait(self):
        for copy in (self.b0, self.b1, self.c0, self.c1):
            copy.wait_recv()


def main_kernel(
    tokens,
    token_tangent,
    gate_weight,
    up_weight,
    gate_delta,
    up_delta,
    down_weight,
    down_delta,
    cotangent,
    primal_out,
    tangent_out,
    input_out,
    hidden_out,
    grad_gate_out,
    grad_up_out,
    tokens_out,
    cotangent_out,
    wide,
    down,
    rows_in,
    cot,
    cot_own,
    cot_pair,
    exact,
    packed,
    first,
    merged,
    from_left,
    from_right,
    z_send,
    z_recv,
    saved,
    whole,
    core_send,
    core_recv,
    y_exact,
    y_packed,
    y_first,
    y_merged,
    y_left,
    y_right,
    dp_send,
    dp_recv,
    swap_send,
    swap_recv,
    result,
    send_sems,
    recv_sems,
    local_sems,
):
    dp, row, col = lax.axis_index("dp"), lax.axis_index("row"), lax.axis_index("col")
    x, zh, y, c = row // 2, row % 2, col // 2, col % 2
    x_right = (dp, lax.rem(x + 1, 4) * 2 + zh, col)
    x_left = (dp, lax.rem(x + 3, 4) * 2 + zh, col)
    y_next = (dp, row, lax.rem(y + 1, 4) * 2 + c)
    y_prev = (dp, row, lax.rem(y + 3, 4) * 2 + c)
    z_far = (dp, x * 2 + (1 - zh), col)
    z_near = (1 - dp, row, col)
    sibling = (dp, row, y * 2 + (1 - c))
    half_rows = rows_in.shape[2]
    block = half_rows // 4
    features = rows_in.shape[3]
    half_features = features // 2
    quarter = half_features // 2
    own_cols = pl.ds(pl.multiple_of(c * half_features, 128), half_features)
    other_cols = pl.ds(pl.multiple_of((1 - c) * half_features, 128), half_features)
    cp = Copies(send_sems, recv_sems, local_sems)

    load_tokens = cp.local(tokens, rows_in.at[0, 0])
    load_cot = cp.local(cotangent, cot_own)
    load_wide = [cp.local(gate_weight, wide.at[0]), cp.local(up_weight, wide.at[1])]
    load_tangent = cp.local(token_tangent, rows_in.at[0, 1])
    load_wide += [cp.local(gate_delta, wide.at[2]), cp.local(up_delta, wide.at[3])]
    load_down = [cp.local(down_weight, down.at[0]), cp.local(down_delta, down.at[1])]

    barrier = pltpu.get_barrier_semaphore()
    partners = (x_right, x_left, y_next, y_prev, z_far, z_near, sibling)
    for device in partners:
        pl.semaphore_signal(barrier, inc=1, device_id=device, device_id_type=MESH)
    pl.semaphore_wait(barrier, len(partners))

    my_part = pl.ds(pl.multiple_of(c * (half_rows // 2), 16), half_rows // 2)

    def send_rows(which):
        return cp.start(rows_in.at[0, which, my_part], rows_in.at[1, which, my_part], z_near)

    def forward_rows(which):
        return cp.start(rows_in.at[1, which, my_part], rows_in.at[1, which, my_part], sibling)

    load_tokens.wait()
    rows_a = send_rows(0)

    small = block // 2
    load_cot.wait()
    my_small = pl.ds(pl.multiple_of(c * small, 8), small)
    cot_pair[my_small] = cot_own[...].astype(F32)
    pair_copy = cp.start(cot_pair.at[my_small], cot_pair.at[my_small], sibling)

    def y_rows(shift):
        return pl.ds(pl.multiple_of(lax.rem(y + shift, 4) * block, 16), block)

    def cot_send(shift, device, cols):
        part = cot.at[0, y_rows(shift), cols]
        return cp.start(part, part, device)

    ring = []
    for unit in range(5):
        ring.append(
            RingSum(
                cp, x, x_left, x_right, block, exact.at[unit], packed.at[unit], first.at[unit],
                merged.at[unit], from_left.at[unit], from_right.at[unit],
            )
        )
    gathers = [RingGather(cp, x, x_left, x_right, block, whole.at[k]) for k in range(4)]

    def store_partial(unit, plane, value):
        exact[unit, plane] = value
        packed[unit, plane] = value.astype(BF16)

    def forward_sums(unit, half):
        for plane in range(2):
            store_partial(unit, plane, dot(rows_in[half, 0], wide[plane]))

    def forward_tangents(unit, half):
        for plane in range(2):
            store_partial(
                unit,
                plane,
                dot(rows_in[half, 0], wide[2 + plane]) + dot(rows_in[half, 1], wide[plane]),
            )

    z_copies = {}

    def finish_x(unit):
        ring[unit].wait()
        for plane in range(2):
            value = ring[unit].total(plane)
            exact[unit, plane, ring[unit].rows(0)] = value
            z_send[unit, plane] = value.astype(z_send.dtype)
        z_copies[unit] = cp.start(z_send.at[unit], z_recv.at[unit], z_far)

    def total(unit, plane):
        return exact[unit, plane, ring[unit].rows(0)] + z_recv[unit, plane].astype(F32)

    def hidden_block(half):
        sums, tangents = 2 * half, 2 * half + 1
        gate_sum, up_sum = total(sums, 0), total(sums, 1)
        gate_tangent, up_tangent = total(tangents, 0), total(tangents, 1)
        logistic = jax.nn.sigmoid(gate_sum)
        activation = gate_sum * logistic
        derivative = logistic * (1.0 + gate_sum * (1.0 - logistic))
        mine = gathers[half].rows(0)
        whole[half, 0, mine] = (activation * up_sum).astype(BF16)
        whole[half, 1, mine] = (
            derivative * gate_tangent * up_sum + activation * up_tangent
        ).astype(BF16)
        saved[half, 0] = up_sum * derivative
        saved[half, 1] = activation
        gathers[half].start()

    def grad_block(half):
        back = total(4, half)
        mine = gathers[2 + half].rows(0)
        whole[2 + half, 0, mine] = (back * saved[half, 0]).astype(BF16)
        whole[2 + half, 1, mine] = (back * saved[half, 1]).astype(BF16)
        gathers[2 + half].start()

    widths = [half_features, half_features, quarter, quarter]
    out_ring, core_copies, dp_copies, swap_copies = {}, {}, {}, {}

    def unit_view(ref, unit):
        return ref.at[unit, :, :, pl.ds(0, widths[unit])]

    def output_part(unit, cols_start):
        half = unit % 2
        cols = pl.ds(pl.multiple_of(cols_start, 128), half_features)
        hidden, hidden_tangent = whole[half, 0], whole[half, 1]
        yield 0, dot(hidden, down[0, :, cols])
        yield 1, dot(hidden_tangent, down[0, :, cols]) + dot(hidden, down[1, :, cols])

    def input_part(unit, cols_start):
        half = unit % 2
        for plane in range(2):
            cols = pl.ds(pl.multiple_of(cols_start + plane * quarter, 128), quarter)
            yield (
                plane,
                dot_trans(whole[2 + half, 0], wide[0, cols])
                + dot_trans(whole[2 + half, 1], wide[1, cols]),
            )

    def out_compute(unit):
        width = widths[unit]
        part = output_part if unit < 2 else input_part
        for plane, value in part(unit, (1 - c) * half_features):
            core_send[unit, plane, :, 0:width] = value
        core_copies[unit] = cp.start(
            unit_view(core_send, unit), unit_view(core_recv, unit), sibling
        )
        for plane, value in part(unit, c * half_features):
            y_exact[unit, plane, :, 0:width] = value

    def out_start(unit):
        width = widths[unit]
        core_copies[unit].wait_recv()
        for plane in range(2):
            value = y_exact[unit, plane, :, 0:width] + core_recv[unit, plane, :, 0:width]
            y_exact[unit, plane, :, 0:width] = value
            y_packed[unit, plane, :, 0:width] = value.astype(BF16)
        views = [unit_view(r, unit) for r in (y_exact, y_packed, y_first, y_merged, y_left, y_right)]
        out_ring[unit] = RingSum(cp, y, y_prev, y_next, block, *views)
        out_ring[unit].start()

    def out_merge(unit):
        out_ring[unit].merge()

    def out_dp(unit):
        width = widths[unit]
        out_ring[unit].wait()
        slot = unit // 2
        for plane in range(2):
            dp_send[slot, plane, :, 0:width] = out_ring[unit].total(plane)
        cols = pl.ds(0, width)
        dp_copies[slot] = cp.start(
            dp_send.at[slot, :, :, cols], dp_recv.at[slot, :, :, cols], z_near
        )

    def out_swap(unit):
        width = widths[unit]
        out_ring[unit].wait()
        slot = unit // 2
        dp_copies[slot].wait_recv()
        for plane in range(2):
            swap_send[slot, plane, :, 0:width] = (
                out_ring[unit].total(plane) + dp_recv[slot, plane, :, 0:width]
            )
        theirs = pl.ds(pl.multiple_of((1 - c) * small, 8), small)
        cols = pl.ds(0, width)
        swap_copies[slot] = cp.start(
            swap_send.at[slot, :, theirs, cols], swap_recv.at[slot, :, :, cols], sibling
        )

    stores = []

    def out_store(unit):
        slot = unit // 2
        swap_copies[slot].wait_recv()
        width = widths[unit]
        for plane in range(2):
            mine = swap_send[slot, plane, my_small, 0:width].astype(BF16)
            other = swap_recv[slot, plane, :, 0:width].astype(BF16)
            if unit < 2:
                result[plane, :, own_cols] = mine
                result[plane, :, other_cols] = other
            else:
                shift = plane * quarter
                result[2, :, pl.ds(pl.multiple_of(c * half_features + shift, 128), width)] = mine
                result[2, :, pl.ds(pl.multiple_of((1 - c) * half_features + shift, 128), width)] = other
        if unit < 2:
            stores.append(cp.local(result.at[0], primal_out))
            stores.append(cp.local(result.at[1], tangent_out))
        else:
            stores.append(cp.local(result.at[2], input_out))

    load_wide[0].wait()
    load_wide[1].wait()
    load_tangent.wait()
    rows_b = send_rows(1)
    forward_sums(0, 0)
    ring[0].start()

    pair_copy.wait_recv()
    cot[0, y_rows(0)] = cot_pair[...].astype(BF16)
    cot_from_prev = cot_send(0, y_next, own_cols)
    cot_from_next = cot_send(0, y_prev, own_cols)

    load_wide[2].wait()
    load_wide[3].wait()
    forward_tangents(1, 0)
    ring[1].start()
    ring[0].merge()

    cot_from_prev.wait_recv()
    cot_far = cot_send(3, y_next, own_cols)
    rows_a.wait_recv()
    rows_c = forward_rows(0)
    cot_from_next.wait_recv()
    cot_far.wait_recv()
    cot_dp = cp.start(cot.at[0, :, own_cols], cot.at[1, :, own_cols], z_near)
    cot_siblings = [cot_send(shift, sibling, own_cols) for shift in (1, 2, 3)]
    rows_c.wait_recv()
    forward_sums(2, 1)
    ring[2].start()
    ring[1].merge()
    finish_x(0)
    rows_b.wait_recv()
    rows_d = forward_rows(1)
    rows_d.wait_recv()
    forward_tangents(3, 1)
    ring[3].start()
    ring[2].merge()
    finish_x(1)

    cot_dp.wait_recv()
    cot_last = cp.start(cot.at[1, :, own_cols], cot.at[1, :, own_cols], sibling)
    for copy in cot_siblings:
        copy.wait_recv()
    load_down[0].wait()
    store_partial(4, 0, dot_trans(cot[0], down[0]))
    cot_last.wait_recv()
    store_partial(4, 1, dot_trans(cot[1], down[0]))
    ring[4].start()
    ring[3].merge()
    z_copies[0].wait_recv()
    z_copies[1].wait_recv()
    hidden_block(0)
    for half in range(2):
        stores.append(cp.local(rows_in.at[half, 0], tokens_out.at[half]))
        stores.append(cp.local(cot.at[half], cotangent_out.at[half]))
    finish_x(2)
    ring[4].merge()
    finish_x(3)
    gathers[0].forward()
    z_copies[2].wait_recv()
    z_copies[3].wait_recv()
    hidden_block(1)
    finish_x(4)
    gathers[0].wait()
    stores.append(cp.local(whole.at[0, 0], hidden_out.at[0]))
    z_copies[4].wait_recv()
    grad_block(1)
    grad_block(0)
    load_down[1].wait()
    out_compute(0)
    gathers[1].forward()
    out_start(0)
    gathers[1].wait()
    stores.append(cp.local(whole.at[1, 0], hidden_out.at[1]))
    out_compute(1)
    gathers[3].forward()
    out_merge(0)
    out_start(1)
    gathers[2].forward()
    out_merge(1)
    gathers[3].wait()
    stores.append(cp.local(whole.at[3, 0], grad_gate_out.at[1]))
    stores.append(cp.local(whole.at[3, 1], grad_up_out.at[1]))
    out_compute(3)
    out_start(3)
    out_dp(1)
    gathers[2].wait()
    stores.append(cp.local(whole.at[2, 0], grad_gate_out.at[0]))
    stores.append(cp.local(whole.at[2, 1], grad_up_out.at[0]))
    out_compute(2)
    out_start(2)
    out_merge(3)
    out_swap(0)
    out_merge(2)
    out_dp(3)
    out_store(0)
    out_swap(2)
    out_store(2)

    for copy in cp.sent:
        copy.wait_send()
    for copy in stores:
        copy.wait()


def gradient_kernel(normalizer, tokens, cotangent, hidden, grad_gate, grad_up, gate_out, up_out, down_out):
    gate_out[...] = (
        lax.dot_general(tokens[...], grad_gate[...], TRANS_LEFT, preferred_element_type=F32)
        * normalizer
    ).astype(BF16)
    up_out[...] = (
        lax.dot_general(tokens[...], grad_up[...], TRANS_LEFT, preferred_element_type=F32)
        * normalizer
    ).astype(BF16)
    down_out[...] = (
        lax.dot_general(hidden[...], cotangent[...], TRANS_LEFT, preferred_element_type=F32)
        * normalizer
    ).astype(BF16)


def on_device(*arguments):
    tokens, _, gate_weight, _, _, _, _, _, cotangent = arguments
    half_rows, features = tokens.shape
    units = gate_weight.shape[1]
    block = half_rows // 4
    half_features = features // 2
    small = cotangent.shape[0]
    shape = jax.ShapeDtypeStruct
    hbm = pl.BlockSpec(memory_space=pl.ANY)
    vm = pltpu.VMEM
    outs = pl.pallas_call(
        main_kernel,
        out_shape=[shape((small, features), BF16)] * 3
        + [shape((2, half_rows, units), BF16)] * 3
        + [shape((2, half_rows, features), BF16)] * 2,
        in_specs=[hbm] * 9,
        out_specs=[hbm] * 8,
        scratch_shapes=[
            vm((4, features, units), BF16),
            vm((2, units, features), BF16),
            vm((2, 2, half_rows, features), BF16),
            vm((2, half_rows, features), BF16),
            vm((small, features), BF16),
            vm((block, features), F32),
            vm((5, 2, half_rows, units), F32),
            vm((5, 2, half_rows, units), BF16),
            vm((5, 2, block, units), BF16),
            vm((5, 2, block, units), BF16),
            vm((5, 2, block, units), BF16),
            vm((5, 2, block, units), BF16),
            vm((5, 2, block, units), BF16),
            vm((5, 2, block, units), BF16),
            vm((2, 2, block, units), F32),
            vm((4, 2, half_rows, units), BF16),
            vm((4, 2, half_rows, half_features), F32),
            vm((4, 2, half_rows, half_features), F32),
            vm((4, 2, half_rows, half_features), F32),
            vm((4, 2, half_rows, half_features), BF16),
            vm((4, 2, block, half_features), BF16),
            vm((4, 2, block, half_features), BF16),
            vm((4, 2, block, half_features), BF16),
            vm((4, 2, block, half_features), BF16),
            vm((2, 2, block, half_features), F32),
            vm((2, 2, block, half_features), F32),
            vm((2, 2, block, half_features), F32),
            vm((2, 2, small, half_features), F32),
            vm((3, small, features), BF16),
            pltpu.SemaphoreType.DMA((120,)),
            pltpu.SemaphoreType.DMA((120,)),
            pltpu.SemaphoreType.DMA((32,)),
        ],
        compiler_params=pltpu.CompilerParams(
            collective_id=0, has_side_effects=True, vmem_limit_bytes=60 << 20
        ),
        cost_estimate=pl.CostEstimate(
            flops=24 * 2 * half_rows * features * units,
            bytes_accessed=12 * features * units,
            transcendentals=0,
        ),
        name="linearized_block",
    )(*arguments)
    primal, tangent, input_cotangent, hidden, grad_gate, grad_up, rows_in, cot = outs
    flat = lambda value: value.reshape(2 * half_rows, value.shape[2])
    vmem = pl.BlockSpec(memory_space=pltpu.VMEM)
    normalizer = 1.0 / math.sqrt(2 * half_rows)
    gate_gradient, up_gradient, down_gradient = pl.pallas_call(
        functools.partial(gradient_kernel, normalizer),
        out_shape=[shape((features, units), BF16)] * 2 + [shape((units, features), BF16)],
        in_specs=[vmem] * 5,
        out_specs=[vmem] * 3,
        compiler_params=pltpu.CompilerParams(vmem_limit_bytes=60 << 20),
        cost_estimate=pl.CostEstimate(
            flops=6 * 2 * half_rows * features * units,
            bytes_accessed=6 * features * units + 16 * half_rows * features,
            transcendentals=0,
        ),
        name="gradients",
    )(flat(rows_in), flat(cot), flat(hidden), flat(grad_gate), flat(grad_up))
    return (primal, tangent, input_cotangent, gate_gradient, up_gradient, down_gradient)


def solution(mesh):
    by_dp = P("dp", "row")
    wide = P("row", ("dp", "col"))
    tall = P(("dp", "col"), "row")
    return jax.shard_map(
        on_device,
        mesh=mesh,
        in_specs=(by_dp, by_dp, wide, wide, wide, wide, tall, tall, tall),
        out_specs=(tall, tall, tall, wide, wide, tall),
        check_vma=False,
    )
```

```python
import functools
import math

import jax
import jax.numpy as jnp
from jax import lax
from jax.experimental import pallas as pl
from jax.experimental.pallas import tpu as pltpu
from jax.sharding import PartitionSpec as P

BF16 = jnp.bfloat16
F32 = jnp.float32
MESH = pl.DeviceIdType.MESH
TRANS_RIGHT = (((1,), (1,)), ((), ()))
TRANS_LEFT = (((0,), (0,)), ((), ()))


def dot(left_side, right_side):
    return jnp.dot(left_side, right_side, preferred_element_type=F32)


def dot_trans(left_side, right_side):
    return lax.dot_general(left_side, right_side, TRANS_RIGHT, preferred_element_type=F32)


class Copies:
    def __init__(self, send_sems, recv_sems, local_sems):
        self.send_sems, self.recv_sems, self.local_sems = send_sems, recv_sems, local_sems
        self.remote_count = 0
        self.local_count = 0
        self.sent = []

    def start(self, src, dst, device):
        k = self.remote_count
        self.remote_count += 1
        copy = pltpu.make_async_remote_copy(
            src_ref=src,
            dst_ref=dst,
            send_sem=self.send_sems.at[k],
            recv_sem=self.recv_sems.at[k],
            device_id=device,
            device_id_type=MESH,
        )
        copy.start()
        self.sent.append(copy)
        return copy

    def local(self, src, dst):
        k = self.local_count
        self.local_count += 1
        copy = pltpu.make_async_copy(src, dst, self.local_sems.at[k])
        copy.start()
        return copy


class RingSum:
    def __init__(self, copies, me, left, right, block, exact, sent, first, merged, from_left, from_right):
        self.copies, self.left, self.right = copies, left, right
        self.rows = lambda shift: pl.ds(pl.multiple_of(lax.rem(me + shift, 4) * block, 16), block)
        self.exact, self.packed, self.first, self.merged = exact, sent, first, merged
        self.from_left, self.from_right = from_left, from_right

    def start(self):
        far, after, before = self.rows(2), self.rows(1), self.rows(3)
        send = self.copies.start
        self.a0 = send(self.packed.at[0, far], self.first.at[0], self.right)
        self.a1 = send(self.packed.at[1, far], self.first.at[1], self.left)
        self.b1 = send(self.packed.at[1, after], self.from_left.at[1], self.right)
        self.b0 = send(self.packed.at[0, before], self.from_right.at[0], self.left)

    def merge(self):
        send = self.copies.start
        self.a0.wait_recv()
        self.merged[0] = (self.exact[0, self.rows(1)] + self.first[0].astype(F32)).astype(self.merged.dtype)
        self.c0 = send(self.merged.at[0], self.from_left.at[0], self.right)
        self.a1.wait_recv()
        self.merged[1] = (self.exact[1, self.rows(3)] + self.first[1].astype(F32)).astype(self.merged.dtype)
        self.c1 = send(self.merged.at[1], self.from_right.at[1], self.left)

    def wait(self):
        for copy in (self.b0, self.b1, self.c0, self.c1):
            copy.wait_recv()

    def total(self, plane):
        return (
            self.exact[plane, self.rows(0)]
            + self.from_left[plane].astype(F32)
            + self.from_right[plane].astype(F32)
        )


class RingGather:
    def __init__(self, copies, me, left, right, block, whole):
        self.copies, self.left, self.right, self.whole = copies, left, right, whole
        self.rows = lambda shift: pl.ds(pl.multiple_of(lax.rem(me + shift, 4) * block, 16), block)

    def send(self, plane, shift, device):
        part = self.whole.at[plane, self.rows(shift)]
        return self.copies.start(part, part, device)

    def start(self):
        self.a0 = self.send(0, 0, self.right)
        self.a1 = self.send(1, 0, self.left)
        self.b1 = self.send(1, 0, self.right)
        self.b0 = self.send(0, 0, self.left)

    def forward(self):
        self.a0.wait_recv()
        self.c0 = self.send(0, 3, self.right)
        self.a1.wait_recv()
        self.c1 = self.send(1, 1, self.left)

    def wait(self):
        for copy in (self.b0, self.b1, self.c0, self.c1):
            copy.wait_recv()


class SplitGather:
    def __init__(self, copies, me, left, right, block, split, whole):
        self.copies, self.left, self.right, self.whole = copies, left, right, whole
        units = whole.shape[1]
        self.parts = (pl.ds(0, split), pl.ds(split, units - split))
        self.rows = lambda shift: pl.ds(pl.multiple_of(lax.rem(me + shift, 4) * block, 16), block)

    def send(self, part, shift, device):
        view = self.whole.at[self.rows(shift), self.parts[part]]
        return self.copies.start(view, view, device)

    def start(self):
        self.a0 = self.send(0, 0, self.right)
        self.a1 = self.send(1, 0, self.left)
        self.b1 = self.send(1, 0, self.right)
        self.b0 = self.send(0, 0, self.left)

    def forward(self):
        self.a0.wait_recv()
        self.c0 = self.send(0, 3, self.right)
        self.a1.wait_recv()
        self.c1 = self.send(1, 1, self.left)

    def wait(self):
        for copy in (self.b0, self.b1, self.c0, self.c1):
            copy.wait_recv()


class PlaneGather:
    def __init__(self, copies, me, left, right, far, plane, block, split, whole):
        self.copies, self.left, self.right, self.far = copies, left, right, far
        self.plane, self.whole = plane, whole
        units = whole.shape[2]
        self.parts = (pl.ds(0, split), pl.ds(split, units - split))
        self.rows = lambda shift: pl.ds(pl.multiple_of(lax.rem(me + shift, 4) * block, 16), block)
        self.crossed = []

    def send(self, part, shift, device):
        view = self.whole.at[self.plane, self.rows(shift), self.parts[part]]
        return self.copies.start(view, view, device)

    def cross(self, part, shift):
        self.crossed.append(self.send(part, shift, self.far))

    def start(self):
        self.a0 = self.send(0, 0, self.right)
        self.a1 = self.send(1, 0, self.left)
        self.b1 = self.send(1, 0, self.right)
        self.b0 = self.send(0, 0, self.left)

    def forward(self):
        self.a0.wait_recv()
        self.c0 = self.send(0, 3, self.right)
        self.cross(0, 3)
        self.a1.wait_recv()
        self.c1 = self.send(1, 1, self.left)
        self.cross(1, 1)

    def forward_far(self):
        self.b1.wait_recv()
        self.cross(1, 3)
        self.b0.wait_recv()
        self.cross(0, 1)
        self.c0.wait_recv()
        self.cross(0, 2)
        self.c1.wait_recv()
        self.cross(1, 2)

    def wait(self):
        for copy in self.crossed:
            copy.wait_recv()


def main_kernel(
    tokens,
    token_tangent,
    gate_weight,
    up_weight,
    gate_delta,
    up_delta,
    down_weight,
    down_delta,
    cotangent,
    primal_out,
    tangent_out,
    input_out,
    hidden_out,
    grad_gate_out,
    grad_up_out,
    tokens_out,
    cotangent_out,
    wide,
    down,
    rows_in,
    cot,
    cot_own,
    cot_pair,
    exact,
    packed,
    first,
    merged,
    from_left,
    from_right,
    z_send,
    z_recv,
    z_wide_send,
    z_wide_recv,
    saved,
    whole,
    core_send,
    core_recv,
    y_exact,
    y_first,
    y_merged,
    y_left,
    y_right,
    y_packed,
    p_first,
    p_merged,
    p_left,
    p_right,
    in_packed,
    in_first,
    in_merged,
    in_left,
    in_right,
    dp_send,
    dp_recv,
    swap_send,
    swap_recv,
    result,
    tokens_turned,
    hidden_turned,
    tangent_base,
    send_sems,
    recv_sems,
    local_sems,
):
    dp, row, col = lax.axis_index("dp"), lax.axis_index("row"), lax.axis_index("col")
    x, zh, y, c = row // 2, row % 2, col // 2, col % 2
    x_right = (dp, lax.rem(x + 1, 4) * 2 + zh, col)
    x_left = (dp, lax.rem(x + 3, 4) * 2 + zh, col)
    y_next = (dp, row, lax.rem(y + 1, 4) * 2 + c)
    y_prev = (dp, row, lax.rem(y + 3, 4) * 2 + c)
    z_far = (dp, x * 2 + (1 - zh), col)
    z_near = (1 - dp, row, col)
    sibling = (dp, row, y * 2 + (1 - c))
    half_rows = rows_in.shape[2]
    block = half_rows // 4
    features = rows_in.shape[3]
    half_features = features // 2
    quarter = half_features // 2
    own_cols = pl.ds(pl.multiple_of(c * half_features, 128), half_features)
    other_cols = pl.ds(pl.multiple_of((1 - c) * half_features, 128), half_features)
    cp = Copies(send_sems, recv_sems, local_sems)

    load_tokens = cp.local(tokens, rows_in.at[0, 0])
    load_cot = cp.local(cotangent, cot_own)
    load_wide = [cp.local(gate_weight, wide.at[0]), cp.local(up_weight, wide.at[1])]
    load_tangent = cp.local(token_tangent, rows_in.at[0, 1])
    load_wide += [cp.local(gate_delta, wide.at[2]), cp.local(up_delta, wide.at[3])]
    load_down = [cp.local(down_weight, down.at[0]), cp.local(down_delta, down.at[1])]

    barrier = pltpu.get_barrier_semaphore()
    partners = (x_right, x_left, y_next, y_prev, z_far, z_near, sibling)
    for device in partners:
        pl.semaphore_signal(barrier, inc=1, device_id=device, device_id_type=MESH)
    pl.semaphore_wait(barrier, len(partners))

    my_part = pl.ds(pl.multiple_of(c * (half_rows // 2), 16), half_rows // 2)

    def send_rows(which):
        return cp.start(rows_in.at[0, which, my_part], rows_in.at[1, which, my_part], z_near)

    def forward_rows(which):
        return cp.start(rows_in.at[1, which, my_part], rows_in.at[1, which, my_part], sibling)

    load_tokens.wait()
    rows_a = send_rows(0)

    small = block // 2
    load_cot.wait()
    my_small = pl.ds(pl.multiple_of(c * small, 8), small)
    cot_pair[my_small] = cot_own[...].astype(F32)
    pair_copy = cp.start(cot_pair.at[my_small], cot_pair.at[my_small], sibling)

    def y_rows(shift):
        return pl.ds(pl.multiple_of(lax.rem(y + shift, 4) * block, 16), block)

    def cot_send(half, shift, device):
        part = cot.at[half, y_rows(shift), own_cols]
        return cp.start(part, part, device)

    def cot_over_dp():
        return cp.start(
            cot.at[0, y_rows(0), own_cols], cot.at[1, y_rows(0), own_cols], z_near
        )

    ring = []
    for unit in range(5):
        ring.append(
            RingSum(
                cp, x, x_left, x_right, block, exact.at[unit], packed.at[unit], first.at[unit],
                merged.at[unit], from_left.at[unit], from_right.at[unit],
            )
        )
    split = (whole.shape[3] // 2 + 127) // 128 * 128
    hidden_gather = RingGather(cp, x, x_left, x_right, block, whole.at[0])
    tangent_gather = [
        SplitGather(cp, x, x_left, x_right, block, split, whole.at[1, half]) for half in range(2)
    ]
    grad_gather = [
        RingGather(cp, x, x_left, x_right, block, whole.at[2]),
        PlaneGather(cp, x, x_left, x_right, z_far, zh, block, split, whole.at[3]),
    ]

    def store_partial(unit, plane, value):
        exact[unit, plane] = value
        packed[unit, plane] = value.astype(BF16)

    def forward_sums(unit, half):
        for plane in range(2):
            store_partial(unit, plane, dot(rows_in[half, 0], wide[plane]))

    def forward_tangents(unit, half):
        for plane in range(2):
            store_partial(
                unit,
                plane,
                dot(rows_in[half, 0], wide[2 + plane]) + dot(rows_in[half, 1], wide[plane]),
            )

    z_copies = {}

    def finish_x(unit):
        ring[unit].wait()
        for plane in range(2):
            value = ring[unit].total(plane)
            exact[unit, plane, ring[unit].rows(0)] = value
            z_refs(unit)[0][plane] = value.astype(z_refs(unit)[0].dtype)
        z_copies[unit] = cp.start(*z_refs(unit), z_far)

    def z_refs(unit):
        if unit in (0, 2):
            return z_wide_send.at[unit // 2], z_wide_recv.at[unit // 2]
        return z_send.at[unit], z_recv.at[unit]

    def total(unit, plane):
        return exact[unit, plane, ring[unit].rows(0)] + z_refs(unit)[1][plane].astype(F32)

    def hidden_block(half):
        gate_sum, up_sum = total(2 * half, 0), total(2 * half, 1)
        logistic = jax.nn.sigmoid(gate_sum)
        activation = gate_sum * logistic
        derivative = logistic * (1.0 + gate_sum * (1.0 - logistic))
        whole[0, half, ring[0].rows(0)] = (activation * up_sum).astype(BF16)
        saved[half, 0] = up_sum * derivative
        saved[half, 1] = activation

    def tangent_block(half):
        unit = 2 * half + 1
        whole[1, half, ring[0].rows(0)] = (
            saved[half, 0] * total(unit, 0) + saved[half, 1] * total(unit, 1)
        ).astype(BF16)
        tangent_gather[half].start()

    def grad_block(half):
        back = total(4, half)
        mine = ring[0].rows(0)
        whole[2 + half, 0, mine] = (back * saved[half, 0]).astype(BF16)
        whole[2 + half, 1, mine] = (back * saved[half, 1]).astype(BF16)
        grad_gather[half].start()

    widths = [half_features, half_features, quarter, quarter]
    out_ring, core_copies, dp_copies, swap_copies = {}, {}, {}, {}

    def unit_view(ref, unit):
        return ref.at[unit, :, :, pl.ds(0, widths[unit])]

    def columns(start, width):
        return pl.ds(pl.multiple_of(start, 128), width)

    def out_part(unit, start):
        width = widths[unit]
        for plane in range(2):
            if unit == 0:
                yield plane, dot(whole[0, plane], down[0, :, columns(start, width)])
            elif unit == 1:
                rows = columns(start, width)
                yield (
                    plane,
                    dot_trans(whole[2 + plane, 0], wide[0, rows])
                    + dot_trans(whole[2 + plane, 1], wide[1, rows]),
                )
            else:
                half = unit - 2
                cols = columns(start + plane * width, width)
                yield (
                    plane,
                    dot(whole[1, half], down[0, :, cols]) + tangent_base[half, :, cols],
                )

    def base_compute(half):
        tangent_base[half] = dot(whole[0, half], down[1])

    def out_compute(unit):
        width = widths[unit]
        for plane, value in out_part(unit, (1 - c) * half_features):
            core_send[unit, plane, :, 0:width] = value
        core_copies[unit] = cp.start(
            unit_view(core_send, unit), unit_view(core_recv, unit), sibling
        )
        for plane, value in out_part(unit, c * half_features):
            y_exact[unit, plane, :, 0:width] = value

    def out_start(unit):
        width = widths[unit]
        core_copies[unit].wait_recv()
        for plane in range(2):
            value = y_exact[unit, plane, :, 0:width] + core_recv[unit, plane, :, 0:width]
            y_exact[unit, plane, :, 0:width] = value
            if unit == 1:
                y_packed[plane] = value.astype(BF16)
            if unit >= 2:
                in_packed[unit - 2, plane] = value.astype(BF16)
        summed = unit_view(y_exact, unit)
        if unit == 0:
            views = [summed, y_first, y_merged, y_left, y_right]
        elif unit == 1:
            views = [y_packed, p_first, p_merged, p_left, p_right]
        else:
            views = [
                r.at[unit - 2] for r in (in_packed, in_first, in_merged, in_left, in_right)
            ]
        out_ring[unit] = RingSum(cp, y, y_prev, y_next, block, summed, *views)
        out_ring[unit].start()

    def out_merge(unit):
        out_ring[unit].merge()

    def out_dp(unit):
        width = widths[unit]
        slot = min(unit, 2)
        out_ring[unit].wait()
        planes = (1,) if unit < 2 else (0, 1)
        for plane in planes:
            dp_send[slot, plane, :, 0:width] = out_ring[unit].total(plane)
        part = pl.ds(planes[0], len(planes))
        cols = pl.ds(0, width)
        dp_copies[slot] = cp.start(
            dp_send.at[slot, part, :, cols], dp_recv.at[slot, part, :, cols], z_near
        )

    theirs = pl.ds(pl.multiple_of((1 - c) * small, 8), small)

    def out_swap(unit):
        width = widths[unit]
        if unit == 2:
            out_ring[unit].wait()
        dp_copies[unit].wait_recv()
        planes = (0,) if unit < 2 else (0, 1)
        for plane in planes:
            swap_send[unit, plane, :, 0:width] = (
                out_ring[unit].total(plane)
                + dp_recv[unit, 1 if unit < 2 else plane, :, 0:width]
            )
        part = pl.ds(0, len(planes))
        cols = pl.ds(0, width)
        swap_copies[unit] = cp.start(
            swap_send.at[unit, part, theirs, cols], swap_recv.at[unit, part, :, cols], sibling
        )

    stores = []

    def out_store(unit):
        swap_copies[unit].wait_recv()
        width = widths[unit]
        for plane in range(1 if unit < 2 else 2):
            mine = columns(c * half_features + plane * width, width)
            other = columns((1 - c) * half_features + plane * width, width)
            result[unit, :, mine] = swap_send[unit, plane, my_small, 0:width].astype(BF16)
            result[unit, :, other] = swap_recv[unit, plane, :, 0:width].astype(BF16)
        outs = (primal_out, input_out, tangent_out)
        stores.append(cp.local(result.at[unit], outs[unit]))

    load_wide[0].wait()
    load_wide[1].wait()
    forward_sums(0, 0)
    ring[0].start()

    pair_copy.wait_recv()
    cot[0, y_rows(0)] = cot_pair[...].astype(BF16)
    cot_cross = cot_over_dp()
    cot_next = [cot_send(0, 0, y_next)]
    cot_prev = [cot_send(0, 0, y_prev)]

    load_tangent.wait()
    load_wide[2].wait()
    load_wide[3].wait()
    forward_tangents(1, 0)
    ring[1].start()
    rows_b = send_rows(1)
    ring[0].merge()
    rows_a.wait_recv()
    rows_c = forward_rows(0)
    cot_next[0].wait_recv()
    cot_far = [cot_send(0, 3, y_next)]
    cot_cross.wait_recv()
    cot_next.append(cot_send(1, 0, y_next))
    cot_prev.append(cot_send(1, 0, y_prev))
    cot_prev[0].wait_recv()
    rows_c.wait_recv()
    forward_sums(2, 1)
    ring[2].start()
    ring[1].merge()
    cot_far[0].wait_recv()
    cot_siblings = [cot_send(0, shift, sibling) for shift in (1, 2, 3)]
    cot_next[1].wait_recv()
    cot_far.append(cot_send(1, 3, y_next))
    finish_x(0)
    for copy in cot_siblings:
        copy.wait_recv()
    load_down[0].wait()
    store_partial(4, 0, dot_trans(cot[0], down[0]))
    rows_b.wait_recv()
    rows_d = forward_rows(1)
    cot_prev[1].wait_recv()
    cot_far[1].wait_recv()
    cot_last = cp.start(cot.at[1, :, own_cols], cot.at[1, :, own_cols], sibling)
    ring[2].merge()
    cot_last.wait_recv()
    store_partial(4, 1, dot_trans(cot[1], down[0]))
    ring[4].start()
    rows_d.wait_recv()
    forward_tangents(3, 1)
    ring[3].start()
    finish_x(2)
    ring[4].merge()
    z_copies[0].wait_recv()
    hidden_block(0)
    tokens_turned[...] = rows_in[:, 0].reshape(2 * half_rows, features).T
    stores.append(cp.local(tokens_turned, tokens_out))
    for half in range(2):
        stores.append(cp.local(cot.at[half], cotangent_out.at[half]))
    ring[3].merge()
    finish_x(4)
    finish_x(3)
    finish_x(1)
    z_copies[2].wait_recv()
    hidden_block(1)
    hidden_gather.start()
    hidden_gather.forward()
    z_copies[4].wait_recv()
    grad_block(1)
    grad_block(0)
    z_copies[3].wait_recv()
    tangent_block(1)
    hidden_gather.wait()
    grad_gather[1].forward()
    load_down[1].wait()
    out_compute(0)
    z_copies[1].wait_recv()
    tangent_block(0)
    grad_gather[1].forward_far()
    out_start(0)
    grad_gather[0].forward()
    base_compute(0)
    tangent_gather[1].forward()
    base_compute(1)
    out_merge(0)
    tangent_gather[0].forward()
    grad_gather[1].wait()
    grad_gather[0].wait()
    out_compute(1)
    out_dp(0)
    tangent_gather[1].wait()
    out_compute(3)
    out_start(1)
    out_start(3)
    tangent_gather[0].wait()
    out_compute(2)
    out_merge(1)
    out_start(2)
    out_merge(3)
    hidden_turned[...] = whole[0].reshape(2 * half_rows, whole.shape[3]).T
    stores.append(cp.local(hidden_turned, hidden_out))
    out_dp(1)
    out_merge(2)
    out_dp(3)
    out_swap(0)
    for half in range(2):
        stores.append(cp.local(whole.at[2 + half, 0], grad_gate_out.at[half]))
        stores.append(cp.local(whole.at[2 + half, 1], grad_up_out.at[half]))
    out_store(0)
    out_swap(1)
    out_swap(2)
    out_store(1)
    out_store(2)

    for copy in cp.sent:
        copy.wait_send()
    for copy in stores:
        copy.wait()


def gradient_kernel(
    normalizer,
    tokens,
    hidden,
    cotangent,
    grad_gate,
    grad_up,
    primal,
    tangent,
    input_cotangent,
    primal_out,
    tangent_out,
    input_out,
    gate_out,
    up_out,
    down_out,
    tokens_in,
    hidden_in,
    cotangent_in,
    gate_in,
    up_in,
    small_in,
    gate_rows,
    up_rows,
    down_rows,
    sems,
):
    copies = []

    def start(src, dst):
        copy = pltpu.make_async_copy(src, dst, sems.at[len(copies)])
        copy.start()
        copies.append(copy)
        return copy

    def piece(rows, pieces):
        return [pl.ds(k * rows // pieces, rows // pieces) for k in range(pieces)]

    load_hidden = start(hidden, hidden_in)
    load_cotangent = start(cotangent, cotangent_in)
    load_tokens = start(tokens, tokens_in)
    load_gate = start(grad_gate, gate_in)
    load_up = start(grad_up, up_in)
    smalls = [start(src, small_in.at[k]) for k, src in enumerate((primal, tangent, input_cotangent))]
    waits = []

    def product(left_side, right_side, rows, out, pieces):
        for part in piece(left_side.shape[0], pieces):
            rows[part] = (dot(left_side[part], right_side[...]) * normalizer).astype(BF16)
            waits.append(start(rows.at[part], out.at[part]))

    load_hidden.wait()
    load_cotangent.wait()
    product(hidden_in, cotangent_in, down_rows, down_out, 2)
    load_tokens.wait()
    load_gate.wait()
    product(tokens_in, gate_in, gate_rows, gate_out, 2)
    for k, dst in enumerate((primal_out, tangent_out, input_out)):
        smalls[k].wait()
        waits.append(start(small_in.at[k], dst))
    load_up.wait()
    product(tokens_in, up_in, up_rows, up_out, 4)
    for copy in waits:
        copy.wait()


def on_device(*arguments):
    tokens, _, gate_weight, _, _, _, _, _, cotangent = arguments
    half_rows, features = tokens.shape
    units = gate_weight.shape[1]
    block = half_rows // 4
    half_features = features // 2
    small = cotangent.shape[0]
    shape = jax.ShapeDtypeStruct
    hbm = pl.BlockSpec(memory_space=pl.ANY)
    vm = pltpu.VMEM
    outs = pl.pallas_call(
        main_kernel,
        out_shape=[shape((small, features), BF16)] * 3
        + [shape((units, 2 * half_rows), BF16)]
        + [shape((2, half_rows, units), BF16)] * 2
        + [shape((features, 2 * half_rows), BF16), shape((2, half_rows, features), BF16)],
        in_specs=[hbm] * 9,
        out_specs=[hbm] * 8,
        scratch_shapes=[
            vm((4, features, units), BF16),
            vm((2, units, features), BF16),
            vm((2, 2, half_rows, features), BF16),
            vm((2, half_rows, features), BF16),
            vm((small, features), BF16),
            vm((block, features), F32),
            vm((5, 2, half_rows, units), F32),
            vm((5, 2, half_rows, units), BF16),
            vm((5, 2, block, units), BF16),
            vm((5, 2, block, units), BF16),
            vm((5, 2, block, units), BF16),
            vm((5, 2, block, units), BF16),
            vm((5, 2, block, units), BF16),
            vm((5, 2, block, units), BF16),
            vm((2, 2, block, units), F32),
            vm((2, 2, block, units), F32),
            vm((2, 2, block, units), F32),
            vm((4, 2, half_rows, units), BF16),
            vm((4, 2, half_rows, half_features), F32),
            vm((4, 2, half_rows, half_features), F32),
            vm((4, 2, half_rows, half_features), F32),
            vm((2, block, half_features), F32),
            vm((2, block, half_features), F32),
            vm((2, block, half_features), F32),
            vm((2, block, half_features), F32),
            vm((2, half_rows, half_features), BF16),
            vm((2, block, half_features), BF16),
            vm((2, block, half_features), BF16),
            vm((2, block, half_features), BF16),
            vm((2, block, half_features), BF16),
            vm((2, 2, half_rows, half_features // 2), BF16),
            vm((2, 2, block, half_features // 2), BF16),
            vm((2, 2, block, half_features // 2), BF16),
            vm((2, 2, block, half_features // 2), BF16),
            vm((2, 2, block, half_features // 2), BF16),
            vm((3, 2, block, half_features), F32),
            vm((3, 2, block, half_features), F32),
            vm((3, 2, block, half_features), F32),
            vm((3, 2, small, half_features), F32),
            vm((3, small, features), BF16),
            vm((features, 2 * half_rows), BF16),
            vm((units, 2 * half_rows), BF16),
            vm((2, half_rows, features), F32),
            pltpu.SemaphoreType.DMA((144,)),
            pltpu.SemaphoreType.DMA((144,)),
            pltpu.SemaphoreType.DMA((32,)),
        ],
        compiler_params=pltpu.CompilerParams(
            collective_id=0, has_side_effects=True, vmem_limit_bytes=60 << 20
        ),
        cost_estimate=pl.CostEstimate(
            flops=24 * 2 * half_rows * features * units,
            bytes_accessed=12 * features * units,
            transcendentals=0,
        ),
        name="linearized_block",
    )(*arguments)
    primal, tangent, input_cotangent, hidden, grad_gate, grad_up, rows_in, cot = outs
    total_rows = 2 * half_rows
    flat = lambda value: value.reshape(total_rows, value.shape[2])
    return pl.pallas_call(
        functools.partial(gradient_kernel, 1.0 / math.sqrt(total_rows)),
        out_shape=[shape((small, features), BF16)] * 3
        + [shape((features, units), BF16)] * 2
        + [shape((units, features), BF16)],
        in_specs=[hbm] * 8,
        out_specs=[hbm] * 6,
        scratch_shapes=[
            vm((features, total_rows), BF16),
            vm((units, total_rows), BF16),
            vm((total_rows, features), BF16),
            vm((total_rows, units), BF16),
            vm((total_rows, units), BF16),
            vm((3, small, features), BF16),
            vm((features, units), BF16),
            vm((features, units), BF16),
            vm((units, features), BF16),
            pltpu.SemaphoreType.DMA((24,)),
        ],
        compiler_params=pltpu.CompilerParams(vmem_limit_bytes=60 << 20),
        cost_estimate=pl.CostEstimate(
            flops=6 * 2 * half_rows * features * units,
            bytes_accessed=6 * features * units + 16 * half_rows * features,
            transcendentals=0,
        ),
        name="gradients",
    )(
        rows_in,
        hidden,
        flat(cot),
        flat(grad_gate),
        flat(grad_up),
        primal,
        tangent,
        input_cotangent,
    )


def solution(mesh):
    by_dp = P("dp", "row")
    wide = P("row", ("dp", "col"))
    tall = P(("dp", "col"), "row")
    return jax.shard_map(
        on_device,
        mesh=mesh,
        in_specs=(by_dp, by_dp, wide, wide, wide, wide, tall, tall, tall),
        out_specs=(tall, tall, tall, wide, wide, tall),
        check_vma=False,
    )
```

```python
import functools
import math

import jax
import jax.numpy as jnp
from jax import lax
from jax.experimental import pallas as pl
from jax.experimental.pallas import tpu as pltpu
from jax.sharding import PartitionSpec as P

BF16 = jnp.bfloat16
F32 = jnp.float32
MESH = pl.DeviceIdType.MESH
TRANS_RIGHT = (((1,), (1,)), ((), ()))
TRANS_LEFT = (((0,), (0,)), ((), ()))


def dot(left_side, right_side):
    return jnp.dot(left_side, right_side, preferred_element_type=F32)


def dot_trans(left_side, right_side):
    return lax.dot_general(left_side, right_side, TRANS_RIGHT, preferred_element_type=F32)


class Copies:
    def __init__(self, send_sems, recv_sems, local_sems):
        self.send_sems, self.recv_sems, self.local_sems = send_sems, recv_sems, local_sems
        self.remote_count = 0
        self.local_count = 0
        self.sent = []

    def start(self, src, dst, device):
        k = self.remote_count
        self.remote_count += 1
        copy = pltpu.make_async_remote_copy(
            src_ref=src,
            dst_ref=dst,
            send_sem=self.send_sems.at[k],
            recv_sem=self.recv_sems.at[k],
            device_id=device,
            device_id_type=MESH,
        )
        copy.start()
        self.sent.append(copy)
        return copy

    def local(self, src, dst):
        k = self.local_count
        self.local_count += 1
        copy = pltpu.make_async_copy(src, dst, self.local_sems.at[k])
        copy.start()
        return copy


class RingSum:
    def __init__(self, copies, me, left, right, block, exact, sent, first, merged, from_left, from_right):
        self.copies, self.left, self.right = copies, left, right
        self.rows = lambda shift: pl.ds(pl.multiple_of(lax.rem(me + shift, 4) * block, 16), block)
        self.exact, self.packed, self.first, self.merged = exact, sent, first, merged
        self.from_left, self.from_right = from_left, from_right

    def start(self):
        far, after, before = self.rows(2), self.rows(1), self.rows(3)
        send = self.copies.start
        self.a0 = send(self.packed.at[0, far], self.first.at[0], self.right)
        self.a1 = send(self.packed.at[1, far], self.first.at[1], self.left)
        self.b1 = send(self.packed.at[1, after], self.from_left.at[1], self.right)
        self.b0 = send(self.packed.at[0, before], self.from_right.at[0], self.left)

    def merge(self):
        send = self.copies.start
        self.a0.wait_recv()
        self.merged[0] = (self.exact[0, self.rows(1)] + self.first[0].astype(F32)).astype(self.merged.dtype)
        self.c0 = send(self.merged.at[0], self.from_left.at[0], self.right)
        self.a1.wait_recv()
        self.merged[1] = (self.exact[1, self.rows(3)] + self.first[1].astype(F32)).astype(self.merged.dtype)
        self.c1 = send(self.merged.at[1], self.from_right.at[1], self.left)

    def wait(self):
        for copy in (self.b0, self.b1, self.c0, self.c1):
            copy.wait_recv()

    def total(self, plane):
        return (
            self.exact[plane, self.rows(0)]
            + self.from_left[plane].astype(F32)
            + self.from_right[plane].astype(F32)
        )


class RingGather:
    def __init__(self, copies, me, left, right, block, whole):
        self.copies, self.left, self.right, self.whole = copies, left, right, whole
        self.rows = lambda shift: pl.ds(pl.multiple_of(lax.rem(me + shift, 4) * block, 16), block)

    def send(self, plane, shift, device):
        part = self.whole.at[plane, self.rows(shift)]
        return self.copies.start(part, part, device)

    def start(self):
        self.a0 = self.send(0, 0, self.right)
        self.a1 = self.send(1, 0, self.left)
        self.b1 = self.send(1, 0, self.right)
        self.b0 = self.send(0, 0, self.left)

    def forward(self):
        self.a0.wait_recv()
        self.c0 = self.send(0, 3, self.right)
        self.a1.wait_recv()
        self.c1 = self.send(1, 1, self.left)

    def wait(self):
        for copy in (self.b0, self.b1, self.c0, self.c1):
            copy.wait_recv()


class SplitGather:
    def __init__(self, copies, me, left, right, block, split, whole):
        self.copies, self.left, self.right, self.whole = copies, left, right, whole
        units = whole.shape[1]
        self.parts = (pl.ds(0, split), pl.ds(split, units - split))
        self.rows = lambda shift: pl.ds(pl.multiple_of(lax.rem(me + shift, 4) * block, 16), block)

    def send(self, part, shift, device):
        view = self.whole.at[self.rows(shift), self.parts[part]]
        return self.copies.start(view, view, device)

    def start(self):
        self.a0 = self.send(0, 0, self.right)
        self.a1 = self.send(1, 0, self.left)
        self.b1 = self.send(1, 0, self.right)
        self.b0 = self.send(0, 0, self.left)

    def forward(self):
        self.a0.wait_recv()
        self.c0 = self.send(0, 3, self.right)
        self.a1.wait_recv()
        self.c1 = self.send(1, 1, self.left)

    def wait(self):
        for copy in (self.b0, self.b1, self.c0, self.c1):
            copy.wait_recv()


class PlaneGather:
    def __init__(self, copies, me, left, right, far, plane, block, split, whole):
        self.copies, self.left, self.right, self.far = copies, left, right, far
        self.plane, self.whole = plane, whole
        units = whole.shape[2]
        self.parts = (pl.ds(0, split), pl.ds(split, units - split))
        self.rows = lambda shift: pl.ds(pl.multiple_of(lax.rem(me + shift, 4) * block, 16), block)
        self.crossed = []

    def send(self, part, shift, device):
        view = self.whole.at[self.plane, self.rows(shift), self.parts[part]]
        return self.copies.start(view, view, device)

    def cross(self, part, shift):
        self.crossed.append(self.send(part, shift, self.far))

    def start(self):
        self.a0 = self.send(0, 0, self.right)
        self.a1 = self.send(1, 0, self.left)
        self.b1 = self.send(1, 0, self.right)
        self.b0 = self.send(0, 0, self.left)

    def forward(self):
        self.a0.wait_recv()
        self.c0 = self.send(0, 3, self.right)
        self.cross(0, 3)
        self.a1.wait_recv()
        self.c1 = self.send(1, 1, self.left)
        self.cross(1, 1)

    def forward_far(self):
        self.b1.wait_recv()
        self.cross(1, 3)
        self.b0.wait_recv()
        self.cross(0, 1)
        self.c0.wait_recv()
        self.cross(0, 2)
        self.c1.wait_recv()
        self.cross(1, 2)

    def wait(self):
        for copy in self.crossed:
            copy.wait_recv()


def main_kernel(
    tokens,
    token_tangent,
    gate_weight,
    up_weight,
    gate_delta,
    up_delta,
    down_weight,
    down_delta,
    cotangent,
    primal_out,
    tangent_out,
    input_out,
    hidden_out,
    grad_gate_out,
    grad_up_out,
    tokens_out,
    cotangent_out,
    wide,
    down,
    rows_in,
    cot,
    cot_own,
    cot_pair,
    exact,
    packed,
    first,
    merged,
    from_left,
    from_right,
    z_send,
    z_recv,
    z_wide_send,
    z_wide_recv,
    saved,
    whole,
    core_send,
    core_recv,
    y_exact,
    y_first,
    y_merged,
    y_left,
    y_right,
    y_packed,
    p_first,
    p_merged,
    p_left,
    p_right,
    in_packed,
    in_first,
    in_merged,
    in_left,
    in_right,
    dp_send,
    dp_recv,
    swap_send,
    swap_recv,
    result,
    tokens_turned,
    hidden_turned,
    tangent_base,
    send_sems,
    recv_sems,
    local_sems,
):
    dp, row, col = lax.axis_index("dp"), lax.axis_index("row"), lax.axis_index("col")
    x, zh, y, c = row // 2, row % 2, col // 2, col % 2
    x_right = (dp, lax.rem(x + 1, 4) * 2 + zh, col)
    x_left = (dp, lax.rem(x + 3, 4) * 2 + zh, col)
    y_next = (dp, row, lax.rem(y + 1, 4) * 2 + c)
    y_prev = (dp, row, lax.rem(y + 3, 4) * 2 + c)
    z_far = (dp, x * 2 + (1 - zh), col)
    z_near = (1 - dp, row, col)
    sibling = (dp, row, y * 2 + (1 - c))
    half_rows = rows_in.shape[2]
    block = half_rows // 4
    features = rows_in.shape[3]
    half_features = features // 2
    quarter = half_features // 2
    own_cols = pl.ds(pl.multiple_of(c * half_features, 128), half_features)
    other_cols = pl.ds(pl.multiple_of((1 - c) * half_features, 128), half_features)
    cp = Copies(send_sems, recv_sems, local_sems)

    load_tokens = cp.local(tokens, rows_in.at[0, 0])
    load_cot = cp.local(cotangent, cot_own)
    load_wide = [cp.local(gate_weight, wide.at[0]), cp.local(up_weight, wide.at[1])]
    load_tangent = cp.local(token_tangent, rows_in.at[0, 1])
    load_wide += [cp.local(gate_delta, wide.at[2]), cp.local(up_delta, wide.at[3])]
    load_down = [cp.local(down_weight, down.at[0]), cp.local(down_delta, down.at[1])]

    barrier = pltpu.get_barrier_semaphore()
    partners = (x_right, x_left, y_next, y_prev, z_far, z_near, sibling)
    for device in partners:
        pl.semaphore_signal(barrier, inc=1, device_id=device, device_id_type=MESH)
    pl.semaphore_wait(barrier, len(partners))

    my_part = pl.ds(pl.multiple_of(c * (half_rows // 2), 16), half_rows // 2)

    def send_rows(which):
        return cp.start(rows_in.at[0, which, my_part], rows_in.at[1, which, my_part], z_near)

    def forward_rows(which):
        return cp.start(rows_in.at[1, which, my_part], rows_in.at[1, which, my_part], sibling)

    load_tokens.wait()
    rows_a = send_rows(0)

    small = block // 2
    load_cot.wait()
    my_small = pl.ds(pl.multiple_of(c * small, 8), small)
    cot_pair[my_small] = cot_own[...].astype(F32)
    pair_copy = cp.start(cot_pair.at[my_small], cot_pair.at[my_small], sibling)

    def y_rows(shift):
        return pl.ds(pl.multiple_of(lax.rem(y + shift, 4) * block, 16), block)

    def cot_send(half, shift, device):
        part = cot.at[half, y_rows(shift), own_cols]
        return cp.start(part, part, device)

    def cot_over_dp():
        return cp.start(
            cot.at[0, y_rows(0), own_cols], cot.at[1, y_rows(0), own_cols], z_near
        )

    ring = []
    for unit in range(5):
        ring.append(
            RingSum(
                cp, x, x_left, x_right, block, exact.at[unit], packed.at[unit], first.at[unit],
                merged.at[unit], from_left.at[unit], from_right.at[unit],
            )
        )
    split = (whole.shape[3] // 2 + 127) // 128 * 128
    hidden_gather = RingGather(cp, x, x_left, x_right, block, whole.at[0])
    tangent_gather = [
        SplitGather(cp, x, x_left, x_right, block, split, whole.at[1, half]) for half in range(2)
    ]
    grad_gather = [
        RingGather(cp, x, x_left, x_right, block, whole.at[2]),
        PlaneGather(cp, x, x_left, x_right, z_far, zh, block, split, whole.at[3]),
    ]

    def store_partial(unit, plane, value):
        exact[unit, plane] = value
        packed[unit, plane] = value.astype(BF16)

    def forward_sums(unit, half):
        for plane in range(2):
            store_partial(unit, plane, dot(rows_in[half, 0], wide[plane]))

    def forward_tangents(unit, half):
        for plane in range(2):
            store_partial(
                unit,
                plane,
                dot(rows_in[half, 0], wide[2 + plane]) + dot(rows_in[half, 1], wide[plane]),
            )

    z_copies = {}

    def finish_x(unit):
        ring[unit].wait()
        for plane in range(2):
            value = ring[unit].total(plane)
            exact[unit, plane, ring[unit].rows(0)] = value
            z_refs(unit)[0][plane] = value.astype(z_refs(unit)[0].dtype)
        z_copies[unit] = cp.start(*z_refs(unit), z_far)

    def z_refs(unit):
        if unit in (0, 2):
            return z_wide_send.at[unit // 2], z_wide_recv.at[unit // 2]
        return z_send.at[unit], z_recv.at[unit]

    def total(unit, plane):
        return exact[unit, plane, ring[unit].rows(0)] + z_refs(unit)[1][plane].astype(F32)

    def hidden_block(half):
        gate_sum, up_sum = total(2 * half, 0), total(2 * half, 1)
        logistic = jax.nn.sigmoid(gate_sum)
        activation = gate_sum * logistic
        derivative = logistic * (1.0 + gate_sum * (1.0 - logistic))
        whole[0, half, ring[0].rows(0)] = (activation * up_sum).astype(BF16)
        saved[half, 0] = up_sum * derivative
        saved[half, 1] = activation

    def tangent_block(half):
        unit = 2 * half + 1
        whole[1, half, ring[0].rows(0)] = (
            saved[half, 0] * total(unit, 0) + saved[half, 1] * total(unit, 1)
        ).astype(BF16)
        tangent_gather[half].start()

    def grad_block(half):
        back = total(4, half)
        mine = ring[0].rows(0)
        whole[2 + half, 0, mine] = (back * saved[half, 0]).astype(BF16)
        whole[2 + half, 1, mine] = (back * saved[half, 1]).astype(BF16)
        grad_gather[half].start()

    widths = [half_features, half_features, quarter, quarter]
    out_ring, core_copies, dp_copies, swap_copies = {}, {}, {}, {}

    def unit_view(ref, unit):
        return ref.at[unit, :, :, pl.ds(0, widths[unit])]

    def columns(start, width):
        return pl.ds(pl.multiple_of(start, 128), width)

    def out_part(unit, start):
        width = widths[unit]
        for plane in range(2):
            if unit == 0:
                yield plane, dot(whole[0, plane], down[0, :, columns(start, width)])
            elif unit == 1:
                rows = columns(start, width)
                yield (
                    plane,
                    dot_trans(whole[2 + plane, 0], wide[0, rows])
                    + dot_trans(whole[2 + plane, 1], wide[1, rows]),
                )
            else:
                half = unit - 2
                cols = columns(start + plane * width, width)
                yield (
                    plane,
                    dot(whole[1, half], down[0, :, cols]) + tangent_base[half, :, cols],
                )

    def base_compute(half):
        tangent_base[half] = dot(whole[0, half], down[1])

    def out_compute(unit):
        width = widths[unit]
        for plane, value in out_part(unit, (1 - c) * half_features):
            core_send[unit, plane, :, 0:width] = value
        core_copies[unit] = cp.start(
            unit_view(core_send, unit), unit_view(core_recv, unit), sibling
        )
        for plane, value in out_part(unit, c * half_features):
            y_exact[unit, plane, :, 0:width] = value

    def out_start(unit):
        width = widths[unit]
        core_copies[unit].wait_recv()
        for plane in range(2):
            value = y_exact[unit, plane, :, 0:width] + core_recv[unit, plane, :, 0:width]
            y_exact[unit, plane, :, 0:width] = value
            if unit == 1:
                y_packed[plane] = value.astype(BF16)
            if unit >= 2:
                in_packed[unit - 2, plane] = value.astype(BF16)
        summed = unit_view(y_exact, unit)
        if unit == 0:
            views = [summed, y_first, y_merged, y_left, y_right]
        elif unit == 1:
            views = [y_packed, p_first, p_merged, p_left, p_right]
        else:
            views = [
                r.at[unit - 2] for r in (in_packed, in_first, in_merged, in_left, in_right)
            ]
        out_ring[unit] = RingSum(cp, y, y_prev, y_next, block, summed, *views)
        out_ring[unit].start()

    def out_merge(unit):
        out_ring[unit].merge()

    def out_dp(unit):
        width = widths[unit]
        slot = min(unit, 2)
        out_ring[unit].wait()
        planes = (1,) if unit < 2 else (0, 1)
        for plane in planes:
            dp_send[slot, plane, :, 0:width] = out_ring[unit].total(plane)
        part = pl.ds(planes[0], len(planes))
        cols = pl.ds(0, width)
        dp_copies[slot] = cp.start(
            dp_send.at[slot, part, :, cols], dp_recv.at[slot, part, :, cols], z_near
        )

    theirs = pl.ds(pl.multiple_of((1 - c) * small, 8), small)

    def out_swap(unit):
        width = widths[unit]
        if unit == 2:
            out_ring[unit].wait()
        dp_copies[unit].wait_recv()
        planes = (0,) if unit < 2 else (0, 1)
        for plane in planes:
            swap_send[unit, plane, :, 0:width] = (
                out_ring[unit].total(plane)
                + dp_recv[unit, 1 if unit < 2 else plane, :, 0:width]
            )
        part = pl.ds(0, len(planes))
        cols = pl.ds(0, width)
        swap_copies[unit] = cp.start(
            swap_send.at[unit, part, theirs, cols], swap_recv.at[unit, part, :, cols], sibling
        )

    stores = []

    def out_store(unit):
        swap_copies[unit].wait_recv()
        width = widths[unit]
        for plane in range(1 if unit < 2 else 2):
            mine = columns(c * half_features + plane * width, width)
            other = columns((1 - c) * half_features + plane * width, width)
            result[unit, :, mine] = swap_send[unit, plane, my_small, 0:width].astype(BF16)
            result[unit, :, other] = swap_recv[unit, plane, :, 0:width].astype(BF16)
        outs = (primal_out, input_out, tangent_out)
        stores.append(cp.local(result.at[unit], outs[unit]))

    def drain(keep):
        while len(cp.sent) > keep:
            cp.sent.pop(0).wait_send()

    load_wide[0].wait()
    load_wide[1].wait()
    forward_sums(0, 0)
    ring[0].start()
    pair_copy.wait_recv()
    cot[0, y_rows(0)] = cot_pair[...].astype(BF16)
    cot_cross = cot_over_dp()
    cot_next = [cot_send(0, 0, y_next)]
    load_tangent.wait()
    load_wide[2].wait()
    load_wide[3].wait()
    forward_tangents(1, 0)
    cot_prev = [cot_send(0, 0, y_prev)]
    rows_b = send_rows(1)
    ring[0].merge()
    rows_a.wait_recv()
    ring[1].start()
    rows_c = forward_rows(0)
    cot_next[0].wait_recv()
    cot_far = [cot_send(0, 3, y_next)]
    cot_cross.wait_recv()
    cot_next.append(cot_send(1, 0, y_next))
    cot_prev.append(cot_send(1, 0, y_prev))
    cot_prev[0].wait_recv()
    rows_c.wait_recv()
    forward_sums(2, 1)
    ring[2].start()
    cot_far[0].wait_recv()
    cot_siblings = [cot_send(0, shift, sibling) for shift in (1, 2, 3)]
    finish_x(0)
    cot_next[1].wait_recv()
    cot_far.append(cot_send(1, 3, y_next))
    for copy in cot_siblings:
        copy.wait_recv()
    load_down[0].wait()
    rows_b.wait_recv()
    store_partial(4, 0, dot_trans(cot[0], down[0]))
    rows_d = forward_rows(1)
    cot_prev[1].wait_recv()
    cot_far[1].wait_recv()
    cot_last = cp.start(cot.at[1, :, own_cols], cot.at[1, :, own_cols], sibling)
    ring[2].merge()
    cot_last.wait_recv()
    store_partial(4, 1, dot_trans(cot[1], down[0]))
    ring[4].start()
    rows_d.wait_recv()
    forward_tangents(3, 1)
    ring[3].start()
    finish_x(2)
    ring[4].merge()
    ring[1].merge()
    z_copies[0].wait_recv()
    hidden_block(0)
    ring[3].merge()
    finish_x(4)
    tokens_turned[...] = rows_in[:, 0].reshape(2 * half_rows, features).T
    drain(24)
    z_copies[2].wait_recv()
    hidden_block(1)
    hidden_gather.start()
    finish_x(3)
    hidden_gather.forward()
    z_copies[4].wait_recv()
    grad_block(1)
    grad_block(0)
    finish_x(1)
    hidden_gather.wait()
    load_down[1].wait()
    hidden_turned[...] = whole[0].reshape(2 * half_rows, whole.shape[3]).T
    drain(16)
    z_copies[3].wait_recv()
    out_compute(0)
    base_compute(0)
    grad_gather[1].forward()
    tangent_block(1)
    out_start(0)
    grad_gather[0].forward()
    for half in range(2):
        stores.append(cp.local(cot.at[half], cotangent_out.at[half]))
    grad_gather[1].forward_far()
    base_compute(1)
    z_copies[1].wait_recv()
    tangent_gather[1].forward()
    tangent_block(0)
    grad_gather[0].wait()
    drain(24)
    out_merge(0)
    grad_gather[1].wait()
    tangent_gather[1].wait()
    out_compute(3)
    out_compute(1)
    out_start(3)
    tangent_gather[0].forward()
    out_dp(0)
    out_start(1)
    out_merge(3)
    tangent_gather[0].wait()
    out_compute(2)
    out_merge(1)
    drain(16)
    out_dp(3)
    out_start(2)
    for half in range(2):
        stores.append(cp.local(whole.at[2 + half, 0], grad_gate_out.at[half]))
        stores.append(cp.local(whole.at[2 + half, 1], grad_up_out.at[half]))
    out_swap(0)
    out_dp(1)
    stores.append(cp.local(tokens_turned, tokens_out))
    drain(12)
    out_merge(2)
    out_swap(2)
    out_swap(1)
    out_store(0)
    out_store(2)
    stores.append(cp.local(hidden_turned, hidden_out))
    out_store(1)

    for copy in cp.sent:
        copy.wait_send()
    for copy in stores:
        copy.wait()


def gradient_kernel(
    normalizer,
    tokens,
    hidden,
    cotangent,
    grad_gate,
    grad_up,
    primal,
    tangent,
    input_cotangent,
    primal_out,
    tangent_out,
    input_out,
    gate_out,
    up_out,
    down_out,
    tokens_in,
    hidden_in,
    cotangent_in,
    gate_in,
    up_in,
    small_in,
    gate_rows,
    up_rows,
    down_rows,
    sems,
):
    copies = []

    def start(src, dst):
        copy = pltpu.make_async_copy(src, dst, sems.at[len(copies)])
        copy.start()
        copies.append(copy)
        return copy

    def piece(rows, pieces):
        return [pl.ds(k * rows // pieces, rows // pieces) for k in range(pieces)]

    load_hidden = start(hidden, hidden_in)
    load_cotangent = start(cotangent, cotangent_in)
    load_tokens = start(tokens, tokens_in)
    load_gate = start(grad_gate, gate_in)
    load_up = start(grad_up, up_in)
    smalls = [start(src, small_in.at[k]) for k, src in enumerate((primal, tangent, input_cotangent))]
    waits = []

    def product(left_side, right_side, rows, out, pieces):
        for part in piece(left_side.shape[0], pieces):
            rows[part] = (dot(left_side[part], right_side[...]) * normalizer).astype(BF16)
            waits.append(start(rows.at[part], out.at[part]))

    load_hidden.wait()
    load_cotangent.wait()
    product(hidden_in, cotangent_in, down_rows, down_out, 2)
    load_tokens.wait()
    load_gate.wait()
    product(tokens_in, gate_in, gate_rows, gate_out, 2)
    for k, dst in enumerate((primal_out, tangent_out, input_out)):
        smalls[k].wait()
        waits.append(start(small_in.at[k], dst))
    load_up.wait()
    product(tokens_in, up_in, up_rows, up_out, 4)
    for copy in waits:
        copy.wait()


def on_device(*arguments):
    tokens, _, gate_weight, _, _, _, _, _, cotangent = arguments
    half_rows, features = tokens.shape
    units = gate_weight.shape[1]
    block = half_rows // 4
    half_features = features // 2
    small = cotangent.shape[0]
    shape = jax.ShapeDtypeStruct
    hbm = pl.BlockSpec(memory_space=pl.ANY)
    vm = pltpu.VMEM
    outs = pl.pallas_call(
        main_kernel,
        out_shape=[shape((small, features), BF16)] * 3
        + [shape((units, 2 * half_rows), BF16)]
        + [shape((2, half_rows, units), BF16)] * 2
        + [shape((features, 2 * half_rows), BF16), shape((2, half_rows, features), BF16)],
        in_specs=[hbm] * 9,
        out_specs=[hbm] * 8,
        scratch_shapes=[
            vm((4, features, units), BF16),
            vm((2, units, features), BF16),
            vm((2, 2, half_rows, features), BF16),
            vm((2, half_rows, features), BF16),
            vm((small, features), BF16),
            vm((block, features), F32),
            vm((5, 2, half_rows, units), F32),
            vm((5, 2, half_rows, units), BF16),
            vm((5, 2, block, units), BF16),
            vm((5, 2, block, units), BF16),
            vm((5, 2, block, units), BF16),
            vm((5, 2, block, units), BF16),
            vm((5, 2, block, units), BF16),
            vm((5, 2, block, units), BF16),
            vm((2, 2, block, units), F32),
            vm((2, 2, block, units), F32),
            vm((2, 2, block, units), F32),
            vm((4, 2, half_rows, units), BF16),
            vm((4, 2, half_rows, half_features), F32),
            vm((4, 2, half_rows, half_features), F32),
            vm((4, 2, half_rows, half_features), F32),
            vm((2, block, half_features), F32),
            vm((2, block, half_features), F32),
            vm((2, block, half_features), F32),
            vm((2, block, half_features), F32),
            vm((2, half_rows, half_features), BF16),
            vm((2, block, half_features), BF16),
            vm((2, block, half_features), BF16),
            vm((2, block, half_features), BF16),
            vm((2, block, half_features), BF16),
            vm((2, 2, half_rows, half_features // 2), BF16),
            vm((2, 2, block, half_features // 2), BF16),
            vm((2, 2, block, half_features // 2), BF16),
            vm((2, 2, block, half_features // 2), BF16),
            vm((2, 2, block, half_features // 2), BF16),
            vm((3, 2, block, half_features), F32),
            vm((3, 2, block, half_features), F32),
            vm((3, 2, block, half_features), F32),
            vm((3, 2, small, half_features), F32),
            vm((3, small, features), BF16),
            vm((features, 2 * half_rows), BF16),
            vm((units, 2 * half_rows), BF16),
            vm((2, half_rows, features), F32),
            pltpu.SemaphoreType.DMA((144,)),
            pltpu.SemaphoreType.DMA((144,)),
            pltpu.SemaphoreType.DMA((32,)),
        ],
        compiler_params=pltpu.CompilerParams(
            collective_id=0, has_side_effects=True, vmem_limit_bytes=60 << 20
        ),
        cost_estimate=pl.CostEstimate(
            flops=24 * 2 * half_rows * features * units,
            bytes_accessed=12 * features * units,
            transcendentals=0,
        ),
        name="linearized_block",
    )(*arguments)
    primal, tangent, input_cotangent, hidden, grad_gate, grad_up, rows_in, cot = outs
    total_rows = 2 * half_rows
    flat = lambda value: value.reshape(total_rows, value.shape[2])
    return pl.pallas_call(
        functools.partial(gradient_kernel, 1.0 / math.sqrt(total_rows)),
        out_shape=[shape((small, features), BF16)] * 3
        + [shape((features, units), BF16)] * 2
        + [shape((units, features), BF16)],
        in_specs=[hbm] * 8,
        out_specs=[hbm] * 6,
        scratch_shapes=[
            vm((features, total_rows), BF16),
            vm((units, total_rows), BF16),
            vm((total_rows, features), BF16),
            vm((total_rows, units), BF16),
            vm((total_rows, units), BF16),
            vm((3, small, features), BF16),
            vm((features, units), BF16),
            vm((features, units), BF16),
            vm((units, features), BF16),
            pltpu.SemaphoreType.DMA((24,)),
        ],
        compiler_params=pltpu.CompilerParams(vmem_limit_bytes=60 << 20),
        cost_estimate=pl.CostEstimate(
            flops=6 * 2 * half_rows * features * units,
            bytes_accessed=6 * features * units + 16 * half_rows * features,
            transcendentals=0,
        ),
        name="gradients",
    )(
        rows_in,
        hidden,
        flat(cot),
        flat(grad_gate),
        flat(grad_up),
        primal,
        tangent,
        input_cotangent,
    )


def solution(mesh):
    by_dp = P("dp", "row")
    wide = P("row", ("dp", "col"))
    tall = P(("dp", "col"), "row")
    return jax.shard_map(
        on_device,
        mesh=mesh,
        in_specs=(by_dp, by_dp, wide, wide, wide, wide, tall, tall, tall),
        out_specs=(tall, tall, tall, wide, wide, tall),
        check_vma=False,
    )
```

```python
import functools
import math

import jax
import jax.numpy as jnp
from jax import lax
from jax.experimental import pallas as pl
from jax.experimental.pallas import tpu as pltpu
from jax.sharding import PartitionSpec as P

BF16 = jnp.bfloat16
F32 = jnp.float32
MESH = pl.DeviceIdType.MESH
TRANS_RIGHT = (((1,), (1,)), ((), ()))
TRANS_LEFT = (((0,), (0,)), ((), ()))


def dot(left_side, right_side):
    return jnp.dot(left_side, right_side, preferred_element_type=F32)


def dot_trans(left_side, right_side):
    return lax.dot_general(left_side, right_side, TRANS_RIGHT, preferred_element_type=F32)


class Copies:
    def __init__(self, send_sems, recv_sems, local_sems):
        self.send_sems, self.recv_sems, self.local_sems = send_sems, recv_sems, local_sems
        self.remote_count = 0
        self.local_count = 0
        self.sent = []

    def start(self, src, dst, device):
        k = self.remote_count
        self.remote_count += 1
        copy = pltpu.make_async_remote_copy(
            src_ref=src,
            dst_ref=dst,
            send_sem=self.send_sems.at[k],
            recv_sem=self.recv_sems.at[k],
            device_id=device,
            device_id_type=MESH,
        )
        copy.start()
        self.sent.append(copy)
        return copy

    def local(self, src, dst):
        k = self.local_count
        self.local_count += 1
        copy = pltpu.make_async_copy(src, dst, self.local_sems.at[k])
        copy.start()
        return copy


class RingSum:
    def __init__(self, copies, me, left, right, block, exact, sent, first, merged, from_left, from_right):
        self.copies, self.left, self.right = copies, left, right
        self.rows = lambda shift: pl.ds(pl.multiple_of(lax.rem(me + shift, 4) * block, 16), block)
        self.exact, self.packed, self.first, self.merged = exact, sent, first, merged
        self.from_left, self.from_right = from_left, from_right

    def start(self):
        far, after, before = self.rows(2), self.rows(1), self.rows(3)
        send = self.copies.start
        self.a0 = send(self.packed.at[0, far], self.first.at[0], self.right)
        self.a1 = send(self.packed.at[1, far], self.first.at[1], self.left)
        self.b1 = send(self.packed.at[1, after], self.from_left.at[1], self.right)
        self.b0 = send(self.packed.at[0, before], self.from_right.at[0], self.left)

    def merge(self):
        send = self.copies.start
        self.a0.wait_recv()
        self.merged[0] = (self.exact[0, self.rows(1)] + self.first[0].astype(F32)).astype(self.merged.dtype)
        self.c0 = send(self.merged.at[0], self.from_left.at[0], self.right)
        self.a1.wait_recv()
        self.merged[1] = (self.exact[1, self.rows(3)] + self.first[1].astype(F32)).astype(self.merged.dtype)
        self.c1 = send(self.merged.at[1], self.from_right.at[1], self.left)

    def wait(self):
        for copy in (self.b0, self.b1, self.c0, self.c1):
            copy.wait_recv()

    def total(self, plane):
        return (
            self.exact[plane, self.rows(0)]
            + self.from_left[plane].astype(F32)
            + self.from_right[plane].astype(F32)
        )


class RingGather:
    def __init__(self, copies, me, left, right, block, whole):
        self.copies, self.left, self.right, self.whole = copies, left, right, whole
        self.rows = lambda shift: pl.ds(pl.multiple_of(lax.rem(me + shift, 4) * block, 16), block)

    def send(self, plane, shift, device):
        part = self.whole.at[plane, self.rows(shift)]
        return self.copies.start(part, part, device)

    def start(self):
        self.a0 = self.send(0, 0, self.right)
        self.a1 = self.send(1, 0, self.left)
        self.b1 = self.send(1, 0, self.right)
        self.b0 = self.send(0, 0, self.left)

    def forward(self):
        self.a0.wait_recv()
        self.c0 = self.send(0, 3, self.right)
        self.a1.wait_recv()
        self.c1 = self.send(1, 1, self.left)

    def wait(self):
        for copy in (self.b0, self.b1, self.c0, self.c1):
            copy.wait_recv()


class SplitGather:
    def __init__(self, copies, me, left, right, block, split, whole):
        self.copies, self.left, self.right, self.whole = copies, left, right, whole
        units = whole.shape[1]
        self.parts = (pl.ds(0, split), pl.ds(split, units - split))
        self.rows = lambda shift: pl.ds(pl.multiple_of(lax.rem(me + shift, 4) * block, 16), block)

    def send(self, part, shift, device):
        view = self.whole.at[self.rows(shift), self.parts[part]]
        return self.copies.start(view, view, device)

    def start(self):
        self.a0 = self.send(0, 0, self.right)
        self.a1 = self.send(1, 0, self.left)
        self.b1 = self.send(1, 0, self.right)
        self.b0 = self.send(0, 0, self.left)

    def forward(self):
        self.a0.wait_recv()
        self.c0 = self.send(0, 3, self.right)
        self.a1.wait_recv()
        self.c1 = self.send(1, 1, self.left)

    def wait(self):
        for copy in (self.b0, self.b1, self.c0, self.c1):
            copy.wait_recv()


class PlaneGather:
    def __init__(self, copies, me, left, right, far, plane, block, split, whole):
        self.copies, self.left, self.right, self.far = copies, left, right, far
        self.plane, self.whole = plane, whole
        units = whole.shape[2]
        self.parts = (pl.ds(0, split), pl.ds(split, units - split))
        self.rows = lambda shift: pl.ds(pl.multiple_of(lax.rem(me + shift, 4) * block, 16), block)
        self.crossed = []

    def send(self, part, shift, device):
        view = self.whole.at[self.plane, self.rows(shift), self.parts[part]]
        return self.copies.start(view, view, device)

    def cross(self, part, shift):
        self.crossed.append(self.send(part, shift, self.far))

    def start(self):
        self.a0 = self.send(0, 0, self.right)
        self.a1 = self.send(1, 0, self.left)
        self.b1 = self.send(1, 0, self.right)
        self.b0 = self.send(0, 0, self.left)

    def forward(self):
        self.a0.wait_recv()
        self.c0 = self.send(0, 3, self.right)
        self.cross(0, 3)
        self.a1.wait_recv()
        self.c1 = self.send(1, 1, self.left)
        self.cross(1, 1)

    def forward_far(self):
        self.b1.wait_recv()
        self.cross(1, 3)
        self.b0.wait_recv()
        self.cross(0, 1)
        self.c0.wait_recv()
        self.cross(0, 2)
        self.c1.wait_recv()
        self.cross(1, 2)

    def wait(self):
        for copy in self.crossed:
            copy.wait_recv()


def main_kernel(
    tokens,
    token_tangent,
    gate_weight,
    up_weight,
    gate_delta,
    up_delta,
    down_weight,
    down_delta,
    cotangent,
    primal_out,
    tangent_out,
    input_out,
    down_gradient,
    grad_gate_out,
    grad_up_out,
    tokens_out,
    wide,
    down,
    rows_in,
    cot,
    cot_own,
    cot_pair,
    exact,
    packed,
    first,
    merged,
    from_left,
    from_right,
    z_send,
    z_recv,
    z_wide_send,
    z_wide_recv,
    saved,
    whole,
    core_send,
    core_recv,
    y_exact,
    y_first,
    y_merged,
    y_left,
    y_right,
    y_packed,
    p_first,
    p_merged,
    p_left,
    p_right,
    in_packed,
    in_first,
    in_merged,
    in_left,
    in_right,
    dp_send,
    dp_recv,
    swap_send,
    swap_recv,
    result,
    tokens_turned,
    down_rows,
    tangent_base,
    send_sems,
    recv_sems,
    local_sems,
):
    dp, row, col = lax.axis_index("dp"), lax.axis_index("row"), lax.axis_index("col")
    x, zh, y, c = row // 2, row % 2, col // 2, col % 2
    x_right = (dp, lax.rem(x + 1, 4) * 2 + zh, col)
    x_left = (dp, lax.rem(x + 3, 4) * 2 + zh, col)
    y_next = (dp, row, lax.rem(y + 1, 4) * 2 + c)
    y_prev = (dp, row, lax.rem(y + 3, 4) * 2 + c)
    z_far = (dp, x * 2 + (1 - zh), col)
    z_near = (1 - dp, row, col)
    sibling = (dp, row, y * 2 + (1 - c))
    half_rows = rows_in.shape[2]
    block = half_rows // 4
    features = rows_in.shape[3]
    half_features = features // 2
    quarter = half_features // 2
    own_cols = pl.ds(pl.multiple_of(c * half_features, 128), half_features)
    other_cols = pl.ds(pl.multiple_of((1 - c) * half_features, 128), half_features)
    cp = Copies(send_sems, recv_sems, local_sems)

    load_tokens = cp.local(tokens, rows_in.at[0, 0])
    load_cot = cp.local(cotangent, cot_own)
    load_wide = [cp.local(gate_weight, wide.at[0]), cp.local(up_weight, wide.at[1])]
    load_tangent = cp.local(token_tangent, rows_in.at[0, 1])
    load_wide += [cp.local(gate_delta, wide.at[2]), cp.local(up_delta, wide.at[3])]
    load_down = [cp.local(down_weight, down.at[0]), cp.local(down_delta, down.at[1])]

    barrier = pltpu.get_barrier_semaphore()
    partners = (x_right, x_left, y_next, y_prev, z_far, z_near, sibling)
    for device in partners:
        pl.semaphore_signal(barrier, inc=1, device_id=device, device_id_type=MESH)
    pl.semaphore_wait(barrier, len(partners))

    my_part = pl.ds(pl.multiple_of(c * (half_rows // 2), 16), half_rows // 2)

    def send_rows(which):
        return cp.start(rows_in.at[0, which, my_part], rows_in.at[1, which, my_part], z_near)

    def forward_rows(which):
        return cp.start(rows_in.at[1, which, my_part], rows_in.at[1, which, my_part], sibling)

    load_tokens.wait()
    rows_a = send_rows(0)

    small = block // 2
    normalizer = 1.0 / math.sqrt(2 * half_rows)
    load_cot.wait()
    my_small = pl.ds(pl.multiple_of(c * small, 8), small)
    cot_pair[my_small] = cot_own[...].astype(F32)
    pair_copy = cp.start(cot_pair.at[my_small], cot_pair.at[my_small], sibling)

    def y_rows(shift):
        return pl.ds(pl.multiple_of(lax.rem(y + shift, 4) * block, 16), block)

    def cot_send(half, shift, device):
        part = cot.at[half, y_rows(shift), own_cols]
        return cp.start(part, part, device)

    def cot_over_dp():
        return cp.start(
            cot.at[0, y_rows(0), own_cols], cot.at[1, y_rows(0), own_cols], z_near
        )

    ring = []
    for unit in range(5):
        ring.append(
            RingSum(
                cp, x, x_left, x_right, block, exact.at[unit], packed.at[unit], first.at[unit],
                merged.at[unit], from_left.at[unit], from_right.at[unit],
            )
        )
    split = (whole.shape[3] // 2 + 127) // 128 * 128
    hidden_gather = RingGather(cp, x, x_left, x_right, block, whole.at[0])
    tangent_gather = [
        SplitGather(cp, x, x_left, x_right, block, split, whole.at[1, half]) for half in range(2)
    ]
    grad_gather = [
        RingGather(cp, x, x_left, x_right, block, whole.at[2]),
        PlaneGather(cp, x, x_left, x_right, z_far, zh, block, split, whole.at[3]),
    ]

    def store_partial(unit, plane, value):
        exact[unit, plane] = value
        packed[unit, plane] = value.astype(BF16)

    def forward_sums(unit, half):
        for plane in range(2):
            store_partial(unit, plane, dot(rows_in[half, 0], wide[plane]))

    def forward_tangents(unit, half):
        for plane in range(2):
            store_partial(
                unit,
                plane,
                dot(rows_in[half, 0], wide[2 + plane]) + dot(rows_in[half, 1], wide[plane]),
            )

    z_copies = {}

    def finish_x(unit):
        ring[unit].wait()
        for plane in range(2):
            value = ring[unit].total(plane)
            exact[unit, plane, ring[unit].rows(0)] = value
            z_refs(unit)[0][plane] = value.astype(z_refs(unit)[0].dtype)
        z_copies[unit] = cp.start(*z_refs(unit), z_far)

    def z_refs(unit):
        if unit in (0, 2):
            return z_wide_send.at[unit // 2], z_wide_recv.at[unit // 2]
        return z_send.at[unit], z_recv.at[unit]

    def total(unit, plane):
        return exact[unit, plane, ring[unit].rows(0)] + z_refs(unit)[1][plane].astype(F32)

    def hidden_block(half):
        gate_sum, up_sum = total(2 * half, 0), total(2 * half, 1)
        logistic = jax.nn.sigmoid(gate_sum)
        activation = gate_sum * logistic
        derivative = logistic * (1.0 + gate_sum * (1.0 - logistic))
        whole[0, half, ring[0].rows(0)] = (activation * up_sum).astype(BF16)
        saved[half, 0] = up_sum * derivative
        saved[half, 1] = activation

    def tangent_block(half):
        unit = 2 * half + 1
        whole[1, half, ring[0].rows(0)] = (
            saved[half, 0] * total(unit, 0) + saved[half, 1] * total(unit, 1)
        ).astype(BF16)
        tangent_gather[half].start()

    def grad_block(half):
        back = total(4, half)
        mine = ring[0].rows(0)
        whole[2 + half, 0, mine] = (back * saved[half, 0]).astype(BF16)
        whole[2 + half, 1, mine] = (back * saved[half, 1]).astype(BF16)
        grad_gather[half].start()

    widths = [half_features, half_features, quarter, quarter]
    out_ring, core_copies, dp_copies, swap_copies = {}, {}, {}, {}

    def unit_view(ref, unit):
        return ref.at[unit, :, :, pl.ds(0, widths[unit])]

    def columns(start, width):
        return pl.ds(pl.multiple_of(start, 128), width)

    def out_part(unit, start):
        width = widths[unit]
        for plane in range(2):
            if unit == 0:
                yield plane, dot(whole[0, plane], down[0, :, columns(start, width)])
            elif unit == 1:
                rows = columns(start, width)
                yield (
                    plane,
                    dot_trans(whole[2 + plane, 0], wide[0, rows])
                    + dot_trans(whole[2 + plane, 1], wide[1, rows]),
                )
            else:
                half = unit - 2
                cols = columns(start + plane * width, width)
                yield (
                    plane,
                    dot(whole[1, half], down[0, :, cols]) + tangent_base[half, :, cols],
                )

    def base_compute(half):
        tangent_base[half] = dot(whole[0, half], down[1])

    def out_compute(unit):
        width = widths[unit]
        for plane, value in out_part(unit, (1 - c) * half_features):
            core_send[unit, plane, :, 0:width] = value
        core_copies[unit] = cp.start(
            unit_view(core_send, unit), unit_view(core_recv, unit), sibling
        )
        for plane, value in out_part(unit, c * half_features):
            y_exact[unit, plane, :, 0:width] = value

    def out_start(unit):
        width = widths[unit]
        core_copies[unit].wait_recv()
        for plane in range(2):
            value = y_exact[unit, plane, :, 0:width] + core_recv[unit, plane, :, 0:width]
            y_exact[unit, plane, :, 0:width] = value
            if unit == 1:
                y_packed[plane] = value.astype(BF16)
            if unit >= 2:
                in_packed[unit - 2, plane] = value.astype(BF16)
        summed = unit_view(y_exact, unit)
        if unit == 0:
            views = [summed, y_first, y_merged, y_left, y_right]
        elif unit == 1:
            views = [y_packed, p_first, p_merged, p_left, p_right]
        else:
            views = [
                r.at[unit - 2] for r in (in_packed, in_first, in_merged, in_left, in_right)
            ]
        out_ring[unit] = RingSum(cp, y, y_prev, y_next, block, summed, *views)
        out_ring[unit].start()

    def out_merge(unit):
        out_ring[unit].merge()

    def out_dp(unit):
        width = widths[unit]
        slot = min(unit, 2)
        out_ring[unit].wait()
        planes = (1,) if unit < 2 else (0, 1)
        for plane in planes:
            dp_send[slot, plane, :, 0:width] = out_ring[unit].total(plane)
        part = pl.ds(planes[0], len(planes))
        cols = pl.ds(0, width)
        dp_copies[slot] = cp.start(
            dp_send.at[slot, part, :, cols], dp_recv.at[slot, part, :, cols], z_near
        )

    theirs = pl.ds(pl.multiple_of((1 - c) * small, 8), small)

    def out_swap(unit):
        width = widths[unit]
        if unit == 2:
            out_ring[unit].wait()
        dp_copies[unit].wait_recv()
        planes = (0,) if unit < 2 else (0, 1)
        for plane in planes:
            swap_send[unit, plane, :, 0:width] = (
                out_ring[unit].total(plane)
                + dp_recv[unit, 1 if unit < 2 else plane, :, 0:width]
            )
        part = pl.ds(0, len(planes))
        cols = pl.ds(0, width)
        swap_copies[unit] = cp.start(
            swap_send.at[unit, part, theirs, cols], swap_recv.at[unit, part, :, cols], sibling
        )

    stores = []

    def out_store(unit):
        swap_copies[unit].wait_recv()
        width = widths[unit]
        for plane in range(1 if unit < 2 else 2):
            mine = columns(c * half_features + plane * width, width)
            other = columns((1 - c) * half_features + plane * width, width)
            result[unit, :, mine] = swap_send[unit, plane, my_small, 0:width].astype(BF16)
            result[unit, :, other] = swap_recv[unit, plane, :, 0:width].astype(BF16)
        outs = (primal_out, input_out, tangent_out)
        stores.append(cp.local(result.at[unit], outs[unit]))

    load_down[0].wait()
    load_wide[0].wait()
    load_wide[1].wait()
    forward_sums(0, 0)
    ring[0].start()
    pair_copy.wait_recv()
    cot[0, y_rows(0)] = cot_pair[...].astype(BF16)
    cot_cross = cot_over_dp()
    cot_next = [cot_send(0, 0, y_next)]
    load_tangent.wait()
    load_wide[2].wait()
    load_wide[3].wait()
    cot_prev = [cot_send(0, 0, y_prev)]
    forward_tangents(1, 0)
    rows_b = send_rows(1)
    ring[0].merge()
    ring[1].start()
    rows_a.wait_recv()
    rows_c = forward_rows(0)
    cot_next[0].wait_recv()
    cot_far = [cot_send(0, 3, y_next)]
    cot_cross.wait_recv()
    cot_next.append(cot_send(1, 0, y_next))
    cot_prev.append(cot_send(1, 0, y_prev))
    cot_prev[0].wait_recv()
    rows_c.wait_recv()
    forward_sums(2, 1)
    ring[2].start()
    cot_far[0].wait_recv()
    cot_siblings = [cot_send(0, shift, sibling) for shift in (1, 2, 3)]
    finish_x(0)
    cot_next[1].wait_recv()
    cot_far.append(cot_send(1, 3, y_next))
    for copy in cot_siblings:
        copy.wait_recv()
    ring[2].merge()
    rows_b.wait_recv()
    rows_d = forward_rows(1)
    cot_prev[1].wait_recv()
    cot_far[1].wait_recv()
    store_partial(4, 0, dot_trans(cot[0], down[0]))
    cot_last = cp.start(cot.at[1, :, own_cols], cot.at[1, :, own_cols], sibling)
    ring[1].merge()
    cot_last.wait_recv()
    tokens_turned[...] = rows_in[:, 0].reshape(2 * half_rows, features).T
    rows_d.wait_recv()
    store_partial(4, 1, dot_trans(cot[1], down[0]))
    ring[4].start()
    finish_x(2)
    ring[4].merge()
    z_copies[0].wait_recv()
    forward_tangents(3, 1)
    ring[3].start()
    finish_x(4)
    hidden_block(0)
    ring[3].merge()
    finish_x(1)
    z_copies[2].wait_recv()
    hidden_block(1)
    hidden_gather.start()
    z_copies[4].wait_recv()
    grad_block(1)
    hidden_gather.forward()
    finish_x(3)
    grad_gather[1].forward()
    z_copies[1].wait_recv()
    grad_block(0)
    hidden_gather.wait()
    out_compute(0)
    hidden_turned = whole[0].reshape(2 * half_rows, whole.shape[3]).T
    down_rows[...] = (
        dot(hidden_turned, cot[...].reshape(2 * half_rows, features)) * normalizer
    ).astype(BF16)
    stores.append(cp.local(down_rows, down_gradient))
    grad_gather[1].forward_far()
    grad_gather[0].forward()
    out_start(0)
    load_down[1].wait()
    z_copies[3].wait_recv()
    tangent_block(1)
    grad_gather[0].wait()
    tangent_block(0)
    tangent_gather[1].forward()
    out_merge(0)
    grad_gather[1].wait()
    out_compute(1)
    base_compute(1)
    tangent_gather[1].wait()
    tangent_gather[0].forward()
    out_start(1)
    stores.append(cp.local(tokens_turned, tokens_out))
    out_compute(3)
    out_dp(0)
    base_compute(0)
    out_start(3)
    tangent_gather[0].wait()
    out_merge(1)
    out_compute(2)
    out_merge(3)
    out_swap(0)
    out_dp(1)
    out_start(2)
    out_dp(3)
    for half in range(2):
        stores.append(cp.local(whole.at[2 + half, 0], grad_gate_out.at[half]))
        stores.append(cp.local(whole.at[2 + half, 1], grad_up_out.at[half]))
    out_merge(2)
    out_store(0)
    out_swap(1)
    out_swap(2)
    out_store(1)
    out_store(2)

    for copy in cp.sent:
        copy.wait_send()
    for copy in stores:
        copy.wait()


def gradient_kernel(
    normalizer,
    tokens,
    down_gradient,
    grad_gate,
    grad_up,
    primal,
    tangent,
    input_cotangent,
    primal_out,
    tangent_out,
    input_out,
    gate_out,
    up_out,
    down_out,
    tokens_in,
    gate_in,
    up_in,
    small_in,
    gate_rows,
    up_rows,
    down_in,
    sems,
):
    copies = []

    def start(src, dst):
        copy = pltpu.make_async_copy(src, dst, sems.at[len(copies)])
        copy.start()
        copies.append(copy)
        return copy

    def piece(rows, pieces):
        return [pl.ds(k * rows // pieces, rows // pieces) for k in range(pieces)]

    load_gate = start(grad_gate, gate_in)
    load_tokens = start(tokens, tokens_in)
    load_up = start(grad_up, up_in)
    load_down = start(down_gradient, down_in)
    smalls = [start(src, small_in.at[k]) for k, src in enumerate((primal, tangent, input_cotangent))]
    waits = []

    def product(left_side, right_side, rows, out, pieces):
        for part in piece(left_side.shape[0], pieces):
            rows[part] = (dot(left_side[part], right_side[...]) * normalizer).astype(BF16)
            waits.append(start(rows.at[part], out.at[part]))

    load_tokens.wait()
    load_gate.wait()
    product(tokens_in, gate_in, gate_rows, gate_out, 4)
    load_down.wait()
    waits.append(start(down_in, down_out))
    for k, dst in enumerate((primal_out, tangent_out, input_out)):
        smalls[k].wait()
        waits.append(start(small_in.at[k], dst))
    load_up.wait()
    product(tokens_in, up_in, up_rows, up_out, 4)
    for copy in waits:
        copy.wait()


def on_device(*arguments):
    tokens, _, gate_weight, _, _, _, _, _, cotangent = arguments
    half_rows, features = tokens.shape
    units = gate_weight.shape[1]
    block = half_rows // 4
    half_features = features // 2
    small = cotangent.shape[0]
    shape = jax.ShapeDtypeStruct
    hbm = pl.BlockSpec(memory_space=pl.ANY)
    vm = pltpu.VMEM
    outs = pl.pallas_call(
        main_kernel,
        out_shape=[shape((small, features), BF16)] * 3
        + [shape((units, features), BF16)]
        + [shape((2, half_rows, units), BF16)] * 2
        + [shape((features, 2 * half_rows), BF16)],
        in_specs=[hbm] * 9,
        out_specs=[hbm] * 7,
        scratch_shapes=[
            vm((4, features, units), BF16),
            vm((2, units, features), BF16),
            vm((2, 2, half_rows, features), BF16),
            vm((2, half_rows, features), BF16),
            vm((small, features), BF16),
            vm((block, features), F32),
            vm((5, 2, half_rows, units), F32),
            vm((5, 2, half_rows, units), BF16),
            vm((5, 2, block, units), BF16),
            vm((5, 2, block, units), BF16),
            vm((5, 2, block, units), BF16),
            vm((5, 2, block, units), BF16),
            vm((5, 2, block, units), BF16),
            vm((5, 2, block, units), BF16),
            vm((2, 2, block, units), F32),
            vm((2, 2, block, units), F32),
            vm((2, 2, block, units), F32),
            vm((4, 2, half_rows, units), BF16),
            vm((4, 2, half_rows, half_features), F32),
            vm((4, 2, half_rows, half_features), F32),
            vm((4, 2, half_rows, half_features), F32),
            vm((2, block, half_features), F32),
            vm((2, block, half_features), F32),
            vm((2, block, half_features), F32),
            vm((2, block, half_features), F32),
            vm((2, half_rows, half_features), BF16),
            vm((2, block, half_features), BF16),
            vm((2, block, half_features), BF16),
            vm((2, block, half_features), BF16),
            vm((2, block, half_features), BF16),
            vm((2, 2, half_rows, half_features // 2), BF16),
            vm((2, 2, block, half_features // 2), BF16),
            vm((2, 2, block, half_features // 2), BF16),
            vm((2, 2, block, half_features // 2), BF16),
            vm((2, 2, block, half_features // 2), BF16),
            vm((3, 2, block, half_features), F32),
            vm((3, 2, block, half_features), F32),
            vm((3, 2, block, half_features), F32),
            vm((3, 2, small, half_features), F32),
            vm((3, small, features), BF16),
            vm((features, 2 * half_rows), BF16),
            vm((units, features), BF16),
            vm((2, half_rows, features), F32),
            pltpu.SemaphoreType.DMA((144,)),
            pltpu.SemaphoreType.DMA((144,)),
            pltpu.SemaphoreType.DMA((32,)),
        ],
        compiler_params=pltpu.CompilerParams(
            collective_id=0, has_side_effects=True, vmem_limit_bytes=60 << 20
        ),
        cost_estimate=pl.CostEstimate(
            flops=24 * 2 * half_rows * features * units,
            bytes_accessed=12 * features * units,
            transcendentals=0,
        ),
        name="linearized_block",
    )(*arguments)
    primal, tangent, input_cotangent, down_gradient, grad_gate, grad_up, rows_in = outs
    total_rows = 2 * half_rows
    flat = lambda value: value.reshape(total_rows, value.shape[2])
    return pl.pallas_call(
        functools.partial(gradient_kernel, 1.0 / math.sqrt(total_rows)),
        out_shape=[shape((small, features), BF16)] * 3
        + [shape((features, units), BF16)] * 2
        + [shape((units, features), BF16)],
        in_specs=[hbm] * 7,
        out_specs=[hbm] * 6,
        scratch_shapes=[
            vm((features, total_rows), BF16),
            vm((total_rows, units), BF16),
            vm((total_rows, units), BF16),
            vm((3, small, features), BF16),
            vm((features, units), BF16),
            vm((features, units), BF16),
            vm((units, features), BF16),
            pltpu.SemaphoreType.DMA((24,)),
        ],
        compiler_params=pltpu.CompilerParams(vmem_limit_bytes=60 << 20),
        cost_estimate=pl.CostEstimate(
            flops=6 * 2 * half_rows * features * units,
            bytes_accessed=6 * features * units + 16 * half_rows * features,
            transcendentals=0,
        ),
        name="gradients",
    )(
        rows_in,
        down_gradient,
        flat(grad_gate),
        flat(grad_up),
        primal,
        tangent,
        input_cotangent,
    )


def solution(mesh):
    by_dp = P("dp", "row")
    wide = P("row", ("dp", "col"))
    tall = P(("dp", "col"), "row")
    return jax.shard_map(
        on_device,
        mesh=mesh,
        in_specs=(by_dp, by_dp, wide, wide, wide, wide, tall, tall, tall),
        out_specs=(tall, tall, tall, wide, wide, tall),
        check_vma=False,
    )
```
